32 devices in a mesh: dp: 4 (over y, x), seq: 4 (over z), mp: 2 (over core).
Axes of the slice: x: 2, y: 2, z: 4, core: 2. Of those that a mesh axis runs over, the one named last changes fastest.
Arguments:
- hidden_in: bfloat16 [4, 1024, 1536], P('dp', 'seq'), may hold values from -6 to 6
- positions: int32 [4, 1024], P('dp', 'seq'), may hold values from 0 to 767, as said below
- mixer_gain: bfloat16 [1536], P(('dp', 'seq')), may hold values from 0.5 to 1.5
- mixer_in: bfloat16 [1536, 3, 1536], P(('dp', 'seq'), None, 'mp'), may hold values from -0.15625 to 0.15625
- mixer_taps: bfloat16 [3, 1536], P(None, 'mp'), may hold values from -3 to 3
- mixer_out: bfloat16 [1536, 1536], P(('dp', 'seq'), 'mp'), may hold values from -0.15625 to 0.15625
- first_gain: bfloat16 [1536], P(('dp', 'seq')), may hold values from 0.5 to 1.5
- first_lift: bfloat16 [1536, 2, 6912], P(('dp', 'seq'), None, 'mp'), may hold values from -0.15625 to 0.15625
- first_drop: bfloat16 [1536, 6912], P(('dp', 'seq'), 'mp'), may hold values from -0.078125 to 0.078125
- attend_gain: bfloat16 [1536], P(('dp', 'seq')), may hold values from 0.5 to 1.5
- query_weight: bfloat16 [1536, 1536], P(('dp', 'seq'), 'mp'), may hold values from -0.15625 to 0.15625
- pair_weight: bfloat16 [1536, 2, 512], P(('dp', 'seq'), None, 'mp'), may hold values from -0.15625 to 0.15625
- query_scale: bfloat16 [64], replicated, may hold values from 0.5 to 1.5
- key_scale: bfloat16 [64], replicated, may hold values from 0.5 to 1.5
- attend_out: bfloat16 [1536, 1536], P(('dp', 'seq'), 'mp'), may hold values from -0.625 to 0.625
- second_gain: bfloat16 [1536], P(('dp', 'seq')), may hold values from 0.5 to 1.5
- second_lift: bfloat16 [1536, 2, 6912], P(('dp', 'seq'), None, 'mp'), may hold values from -0.15625 to 0.15625
- second_drop: bfloat16 [1536, 6912], P(('dp', 'seq'), 'mp'), may hold values from -0.078125 to 0.078125
- cotangent: bfloat16 [4, 1024, 1536], P('dp', 'seq'), may hold values from -6 to 6
Outputs:
- result: bfloat16 [4, 1024, 1536], P('dp', 'seq')
- hidden_gradient: float32 [4, 1024, 1536], P('dp', 'seq')
- mixer_gain_gradient: float32 [1536], P(('dp', 'seq'))
- mixer_in_gradient: float32 [1536, 3, 1536], P(('dp', 'seq'), None, 'mp')
- mixer_taps_gradient: float32 [3, 1536], P(None, 'mp')
- mixer_out_gradient: float32 [1536, 1536], P(('dp', 'seq'), 'mp')
- first_gain_gradient: float32 [1536], P(('dp', 'seq'))
- first_lift_gradient: float32 [1536, 2, 6912], P(('dp', 'seq'), None, 'mp')
- first_drop_gradient: float32 [1536, 6912], P(('dp', 'seq'), 'mp')
- attend_gain_gradient: float32 [1536], P(('dp', 'seq'))
- query_weight_gradient: float32 [1536, 1536], P(('dp', 'seq'), 'mp')
- pair_weight_gradient: float32 [1536, 2, 512], P(('dp', 'seq'), None, 'mp')
- query_scale_gradient: float32 [64], replicated
- key_scale_gradient: float32 [64], replicated
- attend_out_gradient: float32 [1536, 1536], P(('dp', 'seq'), 'mp')
- second_gain_gradient: float32 [1536], P(('dp', 'seq'))
- second_lift_gradient: float32 [1536, 2, 6912], P(('dp', 'seq'), None, 'mp')
- second_drop_gradient: float32 [1536, 6912], P(('dp', 'seq'), 'mp')
The draws below stay inside these ranges and needn't reach their ends.
Inputs may be any that keep to these rules, and one draw needn't show every extreme that they name: In each row three packed documents follow one another, and positions count 0, 1, 2, ... from the start of each: the first and the last have together exactly 256 tokens, each at least one, so the middle one has exactly 768 tokens.
All inputs are finite; a program needn't handle non-finite values.
Results may differ from the reference program's by a relative error of at most 0.035.
Values may be sent and summed in bfloat16 or wider, within the bound.
No kernel may reach another device: no remote copies, remote signals or barrier semaphores. Data moves between devices by JAX's collectives and lax.ppermute only.
A program may use at most 384 MiB of HBM per device.

```python
import jax
import jax.numpy as jnp
from jax import lax

D = 1536
FF = 6912
H = 24
KV = 8
HD = 64
TOK_DEV = 256
SEQS = 4
LENGTH = 1024


def draw_positions(key, part):
    key = jax.random.fold_in(key, 7)
    leading = jax.random.randint(key, (SEQS, 1), 1, TOK_DEV)
    trailing = TOK_DEV - leading
    index = jnp.arange(LENGTH, dtype=jnp.int32)[None, :]
    tail_start = LENGTH - trailing
    inner = jnp.where(index < tail_start, index - leading, index - tail_start)
    return jnp.where(index < leading, index, inner).astype(jnp.int32)


def strengthened(array, stream_key, source, target, parts, factor):
    def block_of(dim):
        return (jnp.arange(array.shape[dim]) // (array.shape[dim] // parts)).reshape((-1,) + (1,) * (array.ndim - 1 - dim))

    first = jax.random.permutation(stream_key, parts)[block_of(target)]
    far = (block_of(target) + parts // 2) % parts
    return jnp.where((block_of(source) == first) | (block_of(source) == far), factor * array, array)


def shard_levels(rng, extent, shards, low, top_value):
    factor_of, own = 1.0, jax.random.fold_in(rng, 6)
    for position, parts in shards:
        heights = jnp.exp(jax.random.uniform(jax.random.fold_in(own, position), (parts,), jnp.float32, low / len(shards), top_value / len(shards)))
        factor_of = factor_of * jnp.repeat(heights, extent[position] // parts).reshape([-1 if axis == position else 1 for axis in range(len(extent))])
    return factor_of


def centred(stream_key, extent, deviation, limit, cuts=(), kind=jnp.bfloat16):
    result = deviation * jax.random.normal(stream_key, extent, jnp.float32)
    if cuts:
        result = result * shard_levels(stream_key, extent, cuts, -0.22, 0.18)
    return jnp.clip(result, -limit, limit).astype(kind)


def bell_draw_with(rng, shape, width, bound, split, heavy, held_as=jnp.bfloat16):
    drawn = width * jax.random.normal(rng, shape, jnp.float32)
    if split:
        drawn = drawn * shard_levels(rng, shape, split, -0.22, 0.18)
    return jnp.clip(strengthened(drawn, jax.random.fold_in(rng, 3), *heavy), -bound, bound).astype(held_as)


def setup_inputs(seed: int = 0) -> dict:
    seeds = jax.random.split(jax.random.key(seed), 20)
    return {
        "hidden_in": centred(seeds[0], (SEQS, LENGTH, D), 1.0, 6.0, ((0, 4), (1, 4))),
        "positions": draw_positions(jax.random.fold_in(seeds[19], 71), 0),
        "mixer_gain": jnp.clip(0.5 + 1.0 * jax.random.uniform(seeds[2], (D,), jnp.float32) ** shard_levels(seeds[2], (D,), ((0, 16),), -0.2, 0.2), 0.5, 1.5).astype(jnp.bfloat16),
        "mixer_in": centred(seeds[3], (D, 3, D), D ** -0.5, 0.15625, ((0, 16), (2, 2))),
        "mixer_taps": centred(seeds[4], (3, D), 0.6, 3.0, ((1, 2),)),
        "mixer_out": centred(seeds[5], (D, D), D ** -0.5, 0.15625, ((0, 16), (1, 2))),
        "first_gain": jnp.clip(0.5 + 1.0 * jax.random.uniform(seeds[6], (D,), jnp.float32) ** shard_levels(seeds[6], (D,), ((0, 16),), -0.2, 0.2), 0.5, 1.5).astype(jnp.bfloat16),
        "first_lift": centred(seeds[7], (D, 2, FF), D ** -0.5, 0.15625, ((0, 16), (2, 2))),
        "first_drop": centred(seeds[8], (D, FF), FF ** -0.5, 0.078125, ((0, 16), (1, 2))),
        "attend_gain": jnp.clip(0.5 + 1.0 * jax.random.uniform(seeds[9], (D,), jnp.float32) ** shard_levels(seeds[9], (D,), ((0, 16),), -0.2, 0.2), 0.5, 1.5).astype(jnp.bfloat16),
        "query_weight": centred(seeds[10], (D, H * HD), D ** -0.5, 0.15625, ((0, 16), (1, 2))),
        "pair_weight": centred(seeds[11], (D, 2, KV * HD), D ** -0.5, 0.15625, ((0, 16), (2, 2))),
        "query_scale": jnp.clip(jax.random.uniform(seeds[12], (HD,), jnp.float32, 0.5, 1.5), 0.5, 1.5).astype(jnp.bfloat16),
        "key_scale": jnp.clip(jax.random.uniform(seeds[13], (HD,), jnp.float32, 0.5, 1.5), 0.5, 1.5).astype(jnp.bfloat16),
        "attend_out": centred(seeds[14], (D, H * HD), (H * HD * 64 // LENGTH) ** -0.5, 0.625, ((0, 16), (1, 2))),
        "second_gain": jnp.clip(0.5 + 1.0 * jax.random.uniform(seeds[15], (D,), jnp.float32) ** shard_levels(seeds[15], (D,), ((0, 16),), -0.2, 0.2), 0.5, 1.5).astype(jnp.bfloat16),
        "second_lift": centred(seeds[16], (D, 2, FF), D ** -0.5, 0.15625, ((0, 16), (2, 2))),
        "second_drop": centred(seeds[17], (D, FF), FF ** -0.5, 0.078125, ((0, 16), (1, 2))),
        "cotangent": bell_draw_with(seeds[18], (SEQS, LENGTH, D), 1.0, 6.0, ((0, 4), (1, 4)), (1, 2, 4, 2.0)),
    }


epsilon = 1e-05
rope_base = 1000000.0
highest = lax.Precision.HIGHEST

@jax.custom_vjp
def low(v):
    return lax.optimization_barrier(v.astype(jnp.bfloat16)).astype(jnp.float32)

@jax.custom_vjp
def low_back(v):
    return v

def low_keep(v):
    return (low(v), None)

def low_pass(kept, grad):
    return (grad,)

def back_keep(v):
    return (v, None)

def back_low(kept, grad):
    return (low(grad),)
low.defvjp(low_keep, low_pass)
low_back.defvjp(back_keep, back_low)

def rms_scale(values):
    return lax.rsqrt(lax.optimization_barrier(jnp.mean(values * values, axis=-1, keepdims=True)) + epsilon)

def frequencies():
    exponent = jnp.arange(HD // 2, dtype=jnp.float32) * (2.0 / HD)
    return jnp.power(rope_base, -exponent)

def rotate(values, cosines, sine_table):
    middle = values.shape[-1] // 2
    leading = values[..., :middle]
    trailing = values[..., middle:]
    return jnp.concatenate([leading * cosines - trailing * sine_table, trailing * cosines + leading * sine_table], axis=-1)

def feed_forward(hidden, gain, lift, drop):
    normed = low(hidden * rms_scale(hidden) * gain)
    gate_up = low_back(jnp.einsum('td,dkf->tkf', normed, lift, precision=highest))
    active = low(jax.nn.silu(gate_up[:, 0]) * gate_up[:, 1])
    return hidden + low_back(jnp.einsum('tf,df->td', active, drop, precision=highest))

def mixer(hidden, token_order, gain, weight_in, tap_values, weight_out):
    normed = low(hidden * rms_scale(hidden) * gain)
    gate_parts = low_back(jnp.einsum('td,dkc->tkc', normed, weight_in, precision=highest))
    gated_input = low(gate_parts[:, 0] * gate_parts[:, 2])
    padded = jnp.concatenate([jnp.zeros((2, gated_input.shape[1]), jnp.float32), gated_input], axis=0)
    one_back = (token_order >= 1).astype(jnp.float32)[:, None]
    two_back = (token_order >= 2).astype(jnp.float32)[:, None]
    convolved = tap_values[2] * padded[2:] + tap_values[1] * padded[1:-1] * one_back + tap_values[0] * padded[:-2] * two_back
    gated_output = low(gate_parts[:, 1] * convolved)
    return hidden + low_back(jnp.einsum('tc,dc->td', gated_output, weight_out, precision=highest))

def attend(hidden, token_order, gain, query_weight, pair_weight, query_scale, key_scale, out_weight):
    normed = low(hidden * rms_scale(hidden) * gain)
    query_heads = low_back(jnp.dot(normed, query_weight, precision=highest)).reshape(LENGTH, H, HD)
    pairs = low_back(jnp.einsum('td,dkc->tkc', normed, pair_weight, precision=highest))
    key_heads = pairs[:, 0].reshape(LENGTH, KV, HD)
    values_low = low(pairs[:, 1]).reshape(LENGTH, KV, HD)
    angles = token_order.astype(jnp.float32)[:, None] * frequencies()[None, :]
    cosines = jnp.cos(angles)[:, None, :]
    sine_table = jnp.sin(angles)[:, None, :]
    query_rot = low(rotate(query_heads * rms_scale(query_heads) * query_scale, cosines, sine_table))
    key_rot = low(rotate(key_heads * rms_scale(key_heads) * key_scale, cosines, sine_table))
    grouped = query_rot.reshape(LENGTH, KV, H // KV, HD)
    span = min(512, LENGTH)
    index = jnp.arange(LENGTH, dtype=jnp.int32)
    doc_first = index - token_order

    def one_block(block_number):
        begin_row = (block_number * span).astype(jnp.int32)
        rows_now = lax.dynamic_slice_in_dim(grouped, begin_row, span, 0)
        row_index = begin_row + jnp.arange(span, dtype=jnp.int32)
        row_first = lax.dynamic_slice_in_dim(doc_first, begin_row, span, 0)
        scores = low_back(jnp.einsum('qgrd,kgd->grqk', rows_now, key_rot, precision=highest) * HD ** (-0.5))
        allowed = (index[None, :] <= row_index[:, None]) & (index[None, :] >= row_first[:, None])
        scores = jnp.where(allowed, scores, -1e+30)
        top_score = lax.optimization_barrier(jnp.max(scores, axis=-1, keepdims=True))
        weights_now = jnp.exp(scores - top_score)
        weights_now = weights_now / lax.optimization_barrier(jnp.sum(weights_now, axis=-1, keepdims=True))
        return jnp.einsum('grqk,kgd->qgrd', low(weights_now), values_low, precision=highest)
    blocks_out = lax.map(jax.checkpoint(one_block), jnp.arange(LENGTH // span, dtype=jnp.int32))
    attended = low_back(low(blocks_out.reshape(LENGTH, H * HD)))
    return hidden + low_back(jnp.einsum('tc,dc->td', attended, out_weight, precision=highest))

def forward(hidden, token_order, params):
    mixer_gain, mixer_in, mixer_taps, mixer_out, first_gain, first_lift, first_drop, attend_gain, query_weight, pair_weight, query_scale, key_scale, attend_out, second_gain, second_lift, second_drop = params
    hidden = mixer(hidden, token_order, mixer_gain, mixer_in, mixer_taps, mixer_out)
    hidden = feed_forward(hidden, first_gain, first_lift, first_drop)
    hidden = attend(hidden, token_order, attend_gain, query_weight, pair_weight, query_scale, key_scale, attend_out)
    return feed_forward(hidden, second_gain, second_lift, second_drop)

def reference(hidden_in, positions, mixer_gain, mixer_in, mixer_taps, mixer_out, first_gain, first_lift, first_drop, attend_gain, query_weight, pair_weight, query_scale, key_scale, attend_out, second_gain, second_lift, second_drop, cotangent):
    params = tuple((weight.astype(jnp.float32) for weight in (mixer_gain, mixer_in, mixer_taps, mixer_out, first_gain, first_lift, first_drop, attend_gain, query_weight, pair_weight, query_scale, key_scale, attend_out, second_gain, second_lift, second_drop)))

    def per_sequence(totals, inputs):
        hidden_row, token_order, seed_row = inputs

        def forward_now(hidden_now, params_now):
            return forward(hidden_now, token_order, params_now)
        result_row, pullback = jax.vjp(forward_now, hidden_row.astype(jnp.float32), params)
        back_row, back_params = pullback(seed_row.astype(jnp.float32))
        totals = jax.tree.map(jnp.add, totals, back_params)
        return (totals, (result_row.astype(jnp.bfloat16), back_row))
    totals, outputs = lax.scan(per_sequence, jax.tree.map(jnp.zeros_like, params), (hidden_in, positions, cotangent))
    return (outputs[0], outputs[1], totals[0], totals[1], totals[2], totals[3], totals[4], totals[5], totals[6], totals[7], totals[8], totals[9], totals[10], totals[11], totals[12], totals[13], totals[14], totals[15])
```

```python
import jax
import jax.numpy as jnp
from jax import lax
from jax.sharding import PartitionSpec as P

HD = 64
GRID = ("dp", "seq")
SEATS = ((0, 0), (0, 1), (1, 0), (1, 1))

epsilon = 1e-05
rope_base = 1000000.0
bf16 = jnp.bfloat16
f32 = jnp.float32


def rms_scale(values):
    return lax.rsqrt(jnp.mean(values * values, axis=-1, keepdims=True) + epsilon)


def norm_back(back_normed, normed, inverse):
    return inverse * (back_normed - normed * jnp.mean(back_normed * normed, axis=-1, keepdims=True))


def frequencies():
    exponent = jnp.arange(HD // 2, dtype=f32) * (2.0 / HD)
    return jnp.power(rope_base, -exponent)


def rotate(values, cosines, sine_table):
    middle = values.shape[-1] // 2
    leading = values[..., :middle]
    trailing = values[..., middle:]
    return jnp.concatenate(
        [leading * cosines - trailing * sine_table, trailing * cosines + leading * sine_table],
        axis=-1,
    )


def dot(pattern, first, second):
    return jnp.einsum(pattern, first, second, preferred_element_type=f32)


class Place:
    def __init__(self):
        dp, seq = lax.axis_index("dp"), lax.axis_index("seq")
        self.core = lax.axis_index("mp")
        self.u, self.v = dp // 2, dp % 2
        self.g, self.w = seq // 2, seq % 2
        self.seat = 2 * self.v + self.w
        self.rank = dp * lax.axis_size("seq") + seq


def far_groups():
    return lax.axis_size("seq") // 2


def swap(array, dp_mask, seq_mask):
    dps, seqs = lax.axis_size("dp"), lax.axis_size("seq")
    pairs = [
        (d * seqs + s, (d ^ dp_mask) * seqs + (s ^ seq_mask)) for d in range(dps) for s in range(seqs)
    ]
    return lax.ppermute(array, GRID, pairs)


def swap_core(array):
    return lax.ppermute(array, "mp", [(0, 1), (1, 0)])


def shift_groups(array, by, cyclic=False):
    seqs = lax.axis_size("seq")
    if cyclic:
        pairs = [(s, (s + 2 * by) % seqs) for s in range(seqs)]
    else:
        pairs = [(s, s + 2 * by) for s in range(seqs) if 0 <= s + 2 * by < seqs]
    return lax.ppermute(array, "seq", pairs)


def flip_if(bit, array, axis):
    return jnp.where(bit == 1, jnp.flip(array, axis), array)


def gather_tokens(own):
    mine = jnp.stack([own] + [swap(own, v, w) for v, w in SEATS[1:]])
    other = swap_core(mine)
    return jnp.stack([mine, other])


def gather_flat(own):
    return gather_tokens(own).reshape(-1, own.shape[-1])


def scatter_tokens(partial_sum):
    rows = partial_sum.shape[0] // 8
    split = partial_sum.reshape(2, 4, rows, partial_sum.shape[-1])
    both = split[0] + swap_core(split[1].astype(bf16)).astype(f32)
    low = both.astype(bf16)
    total = both[0]
    for seat in range(1, 4):
        total = total + swap(low[seat], *SEATS[seat]).astype(f32)
    return total


def in_order(place, flat):
    columns = flat.shape[-1]
    rows = flat.shape[0] // 8
    split = flat.reshape(2, 2, 2, rows, columns)
    split = flip_if(place.w, flip_if(place.core, split, 0), 2)
    return split.transpose(1, 2, 0, 3, 4).reshape(2, 4 * rows, columns)


def own_order(place, ordered):
    columns = ordered.shape[-1]
    rows = ordered.shape[1] // 4
    split = ordered.reshape(2, 2, 2, rows, columns).transpose(2, 0, 1, 3, 4)
    split = flip_if(place.w, flip_if(place.core, split, 0), 2)
    return split.reshape(8 * rows, columns)


def spread_weights(place, packed):
    far = far_groups()
    lead, rows, columns = packed.shape[1:-2], packed.shape[-2], packed.shape[-1]
    plain = (0,) * len(lead)

    def chunk(seat):
        return lax.dynamic_index_in_dim(packed, place.seat ^ seat, 0, keepdims=False)

    near = jnp.zeros(lead + (2, 2, rows, columns), packed.dtype)
    for seat, (v, w) in enumerate(SEATS):
        piece = chunk(seat)
        if seat:
            piece = swap(piece, v, w)
        near = lax.dynamic_update_slice(
            near, piece.reshape(lead + (1, 1, rows, columns)), plain + (place.v ^ v, place.w ^ w, 0, 0)
        )
    whole = jnp.zeros(lead + (2, 2, far, 2, rows, columns), packed.dtype)
    for step in range(far):
        piece = shift_groups(near, step, cyclic=True) if step else near
        opposite = swap(piece, 2, 0)
        group = (place.g - step) % far
        for u, part in ((place.u, piece), (place.u ^ 1, opposite)):
            whole = lax.dynamic_update_slice(
                whole,
                part.reshape(lead + (1, 2, 1, 2, rows, columns)),
                plain + (u, 0, group, 0, 0, 0),
            )
    return whole.reshape(lead + (4 * far * 2 * rows, columns))


def collect_gradient(place, gradient):
    far = far_groups()
    lead, columns = gradient.shape[:-2], gradient.shape[-1]
    rows = gradient.shape[-2] // (8 * far)
    at = len(lead)
    split = gradient.reshape(lead + (2, 2, far, 2, rows, columns))

    def pick(array, index, axis):
        return lax.dynamic_index_in_dim(array, index, axis, keepdims=False)

    send = pick(split, place.u ^ 1, at).astype(bf16)
    half = pick(split, place.u, at).astype(f32) + swap(send, 2, 0).astype(f32)
    part = pick(half, place.g, at + 1)
    for step in range(1, far):
        send = pick(half, (place.g + step) % far, at + 1).astype(bf16)
        part = part + shift_groups(send, step, cyclic=True).astype(f32)
    part = part.astype(bf16)
    pieces = []
    for v, w in SEATS:
        piece = pick(pick(part, place.v ^ v, at), place.w ^ w, at)
        pieces.append(swap(piece, v, w) if v or w else piece)
    seats = jnp.stack(pieces).reshape((2, 2) + lead + (rows, columns))
    seats = flip_if(place.w, flip_if(place.v, seats, 0), 1)
    return seats.reshape((4,) + lead + (rows, columns)).astype(f32)


def per_seat(array):
    split = array.reshape(array.shape[:-1] + (4, array.shape[-1] // 4))
    return jnp.moveaxis(split, -2, 0)


def all_seats(array):
    split = jnp.moveaxis(array, 0, -2)
    return split.reshape(split.shape[:-2] + (-1,))


def pack_mixer(weight_in, weight_out):
    rows = weight_in.shape[0]
    return jnp.concatenate([per_seat(weight_in).reshape(4, rows, -1), per_seat(weight_out)], axis=-1)


def pack_attend(query_weight, pair_weight, out_weight):
    rows = query_weight.shape[0]
    return jnp.concatenate(
        [per_seat(query_weight), per_seat(pair_weight).reshape(4, rows, -1), per_seat(out_weight)], axis=-1
    )


def pack_forward(lift, drop):
    return jnp.concatenate([per_seat(lift).transpose(0, 2, 1, 3), per_seat(drop)[:, None]], axis=1)


def lowered_norm(hidden, gain):
    inverse = rms_scale(hidden)
    normed = hidden * inverse
    return inverse, normed, (normed * gain).astype(bf16)


def feed_forward(hidden, gain, weights):
    inverse, normed, lowered = lowered_norm(hidden, gain)
    tokens = gather_flat(lowered)
    gate = dot("td,df->tf", tokens, weights[0])
    up = dot("td,df->tf", tokens, weights[1])
    active = (jax.nn.silu(gate) * up).astype(bf16)
    out = scatter_tokens(dot("tf,df->td", active, weights[2]))
    return hidden + out, (inverse, normed, tokens, gate, up, active)


def feed_backward(back_out, stored, gain, weights):
    inverse, normed, tokens, gate, up, active = stored
    back_tokens = gather_flat(back_out.astype(bf16))
    back_active = dot("td,df->tf", back_tokens, weights[2])
    sigmoid_value = jax.nn.sigmoid(gate)
    back_gate = (
        back_active * up * sigmoid_value * (1.0 + gate * (1.0 - sigmoid_value))
    ).astype(bf16)
    back_up = (back_active * gate * sigmoid_value).astype(bf16)
    back_normed = scatter_tokens(
        dot("tf,df->td", back_gate, weights[0]) + dot("tf,df->td", back_up, weights[1])
    )
    drop_term = dot("td,tf->df", back_tokens, active)
    lift_terms = (dot("td,tf->df", tokens, back_gate), dot("td,tf->df", tokens, back_up))
    gain_term = jnp.sum(back_normed * normed, axis=0)
    back_hidden = back_out + norm_back(back_normed * gain, normed, inverse)
    return back_hidden, gain_term, jnp.stack(lift_terms + (drop_term,)).astype(bf16)


def mixer_forward(place, hidden, order, gain, weights, taps):
    inverse, normed, lowered = lowered_norm(hidden, gain)
    tokens = gather_flat(lowered)
    channels = taps.shape[1]
    parts = in_order(place, dot("td,dc->tc", tokens, weights[:, : 3 * channels]))
    gate_in, gate_out, value = (parts[..., i * channels : (i + 1) * channels] for i in range(3))
    mixed = (gate_in * value).astype(bf16)
    earlier = shift_groups(mixed[:, -2:], 1)
    padded = jnp.concatenate([earlier, mixed], axis=1).astype(f32)
    one_back = (order >= 1).astype(f32)[..., None]
    two_back = (order >= 2).astype(f32)[..., None]
    convolved = (
        taps[2] * padded[:, 2:] + taps[1] * padded[:, 1:-1] * one_back + taps[0] * padded[:, :-2] * two_back
    )
    gated = own_order(place, (gate_out * convolved).astype(bf16))
    out = scatter_tokens(dot("tc,dc->td", gated, weights[:, 3 * channels :]))
    stored = (inverse, normed, tokens, gate_in, gate_out, value, padded, convolved, gated, one_back, two_back)
    return hidden + out, stored


def mixer_backward(place, back_out, stored, gain, weights, taps):
    inverse, normed, tokens, gate_in, gate_out, value, padded, convolved, gated, one_back, two_back = stored
    channels = taps.shape[1]
    back_tokens = gather_flat(back_out.astype(bf16))
    back_gated = in_order(place, dot("td,dc->tc", back_tokens, weights[:, 3 * channels :]))
    out_term = dot("td,tc->dc", back_tokens, gated)
    back_conv = back_gated * gate_out
    tap_term = jnp.stack(
        [
            jnp.sum(back_conv * padded[:, :-2] * two_back, axis=(0, 1)),
            jnp.sum(back_conv * padded[:, 1:-1] * one_back, axis=(0, 1)),
            jnp.sum(back_conv * padded[:, 2:], axis=(0, 1)),
        ]
    )
    back_padded = (
        jnp.pad(taps[2] * back_conv, ((0, 0), (2, 0), (0, 0)))
        + jnp.pad(taps[1] * back_conv * one_back, ((0, 0), (1, 1), (0, 0)))
        + jnp.pad(taps[0] * back_conv * two_back, ((0, 0), (0, 2), (0, 0)))
    )
    later = shift_groups(back_padded[:, :2], -1)
    back_mixed = back_padded[:, 2:] + jnp.pad(later, ((0, 0), (back_conv.shape[1] - 2, 0), (0, 0)))
    back_parts = own_order(
        place,
        jnp.concatenate([back_mixed * value, back_gated * convolved, back_mixed * gate_in], axis=-1).astype(bf16),
    )
    back_normed = scatter_tokens(dot("tc,dc->td", back_parts, weights[:, : 3 * channels]))
    in_term = dot("td,tc->dc", tokens, back_parts)
    gain_term = jnp.sum(back_normed * normed, axis=0)
    back_hidden = back_out + norm_back(back_normed * gain, normed, inverse)
    return back_hidden, gain_term, jnp.concatenate([in_term, out_term], axis=-1).astype(bf16), tap_term


def attend_forward(place, hidden, order, gain, weights, query_gain, key_gain):
    inverse, normed, lowered = lowered_norm(hidden, gain)
    tokens = gather_flat(lowered)
    heads = weights.shape[1] * 3 // 8 // HD
    groups = weights.shape[1] // 8 // HD
    repeat = heads // groups
    mixed = in_order(place, dot("td,dc->tc", tokens, weights[:, : (heads + 2 * groups) * HD]))
    sequences, count = mixed.shape[:2]
    query_heads = mixed[..., : heads * HD].reshape(sequences, count, heads, HD)
    key_heads = mixed[..., heads * HD : (heads + groups) * HD].reshape(sequences, count, groups, HD)
    value_low = mixed[..., (heads + groups) * HD :].astype(bf16)
    angles = order.astype(f32)[..., None] * frequencies()
    cosines, sines = jnp.cos(angles)[:, :, None, :], jnp.sin(angles)[:, :, None, :]
    query_inverse = rms_scale(query_heads)
    query_normed = query_heads * query_inverse
    query_rot = rotate(query_normed * query_gain, cosines, sines).astype(bf16)
    key_inverse = rms_scale(key_heads)
    key_normed = key_heads * key_inverse
    key_rot = rotate(key_normed * key_gain, cosines, sines).astype(bf16)
    pair = jnp.concatenate([key_rot.reshape(sequences, count, groups * HD), value_low], axis=-1)
    slots = jnp.concatenate([shift_groups(pair, i) if i else pair for i in range(far_groups())], axis=1)
    keys = slots[..., : groups * HD].reshape(sequences, -1, groups, HD)
    values = slots[..., groups * HD :].reshape(sequences, -1, groups, HD)
    grouped = query_rot.reshape(sequences, count, groups, repeat, HD)
    row_index = place.g * count + jnp.arange(count, dtype=jnp.int32)
    row_first = row_index[None] - order
    key_index = jnp.concatenate(
        [(place.g - i) * count + jnp.arange(count, dtype=jnp.int32) for i in range(far_groups())]
    )
    allowed = (key_index[None, None, :] <= row_index[None, :, None]) & (
        key_index[None, None, :] >= row_first[:, :, None]
    )
    scores = dot("vqgrd,vkgd->vgrqk", grouped, keys) * HD**-0.5
    scores = jnp.where(allowed[:, None, None], scores, -1e30)
    probs = jnp.exp(scores - jnp.max(scores, axis=-1, keepdims=True))
    probs = probs / jnp.sum(probs, axis=-1, keepdims=True)
    attended = dot("vgrqk,vkgd->vqgrd", probs.astype(bf16), values).astype(bf16)
    attended = own_order(place, attended.reshape(sequences, count, heads * HD))
    out = scatter_tokens(dot("tc,dc->td", attended, weights[:, (heads + 2 * groups) * HD :]))
    stored = (
        inverse,
        normed,
        tokens,
        query_inverse,
        query_normed,
        key_inverse,
        key_normed,
        cosines,
        sines,
        grouped,
        keys,
        values,
        probs,
        attended,
    )
    return hidden + out, stored


def attend_backward(place, back_out, stored, gain, weights, query_gain, key_gain):
    (
        inverse,
        normed,
        tokens,
        query_inverse,
        query_normed,
        key_inverse,
        key_normed,
        cosines,
        sines,
        grouped,
        keys,
        values,
        probs,
        attended,
    ) = stored
    sequences, count, groups, repeat = grouped.shape[:4]
    heads = groups * repeat
    inner = (heads + 2 * groups) * HD
    back_tokens = gather_flat(back_out.astype(bf16))
    back_attended = in_order(place, dot("td,dc->tc", back_tokens, weights[:, inner:]).astype(bf16))
    back_grouped = back_attended.reshape(sequences, count, groups, repeat, HD)
    out_term = dot("td,tc->dc", back_tokens, attended)
    back_probs = dot("vqgrd,vkgd->vgrqk", back_grouped, values)
    row_dot = jnp.sum(probs * back_probs, axis=-1, keepdims=True)
    back_scores = (probs * (back_probs - row_dot)).astype(bf16)
    back_query_rot = dot("vgrqk,vkgd->vqgrd", back_scores, keys) * HD**-0.5
    back_keys = dot("vgrqk,vqgrd->vkgd", back_scores, grouped) * HD**-0.5
    back_values = dot("vgrqk,vqgrd->vkgd", probs.astype(bf16), back_grouped)
    back_slots = jnp.concatenate(
        [
            back_keys.reshape(sequences, -1, count, groups * HD),
            back_values.reshape(sequences, -1, count, groups * HD),
        ],
        axis=-1,
    )
    back_pair = back_slots[:, 0]
    for i in range(1, far_groups()):
        back_pair = back_pair + shift_groups(back_slots[:, i].astype(bf16), -i).astype(f32)
    back_query_scaled = rotate(back_query_rot.reshape(sequences, count, heads, HD), cosines, -sines)
    query_scale_term = jnp.sum(back_query_scaled * query_normed, axis=(0, 1, 2))
    back_query = norm_back(back_query_scaled * query_gain, query_normed, query_inverse)
    back_key_rot = back_pair[..., : groups * HD].reshape(sequences, count, groups, HD)
    back_key_scaled = rotate(back_key_rot, cosines, -sines)
    key_scale_term = jnp.sum(back_key_scaled * key_normed, axis=(0, 1, 2))
    back_key = norm_back(back_key_scaled * key_gain, key_normed, key_inverse)
    back_mixed = jnp.concatenate(
        [
            back_query.reshape(sequences, count, heads * HD),
            back_key.reshape(sequences, count, groups * HD),
            back_pair[..., groups * HD :],
        ],
        axis=-1,
    ).astype(bf16)
    back_mixed = own_order(place, back_mixed)
    back_normed = scatter_tokens(dot("tc,dc->td", back_mixed, weights[:, :inner]))
    in_term = dot("td,tc->dc", tokens, back_mixed)
    gain_term = jnp.sum(back_normed * normed, axis=0)
    back_hidden = back_out + norm_back(back_normed * gain, normed, inverse)
    return (
        back_hidden,
        gain_term,
        jnp.concatenate([in_term, out_term], axis=-1).astype(bf16),
        (query_scale_term, key_scale_term),
    )


def grid_total(array):
    for mask in (1, 2):
        array = array + swap(array, mask, 0)
    mask = 1
    while mask < lax.axis_size("seq"):
        array = array + swap(array, 0, mask)
        mask *= 2
    return array


def body(
    hidden_in,
    positions,
    mixer_gain,
    mixer_in,
    mixer_taps,
    mixer_out,
    first_gain,
    first_lift,
    first_drop,
    attend_gain,
    query_weight,
    pair_weight,
    query_scale,
    key_scale,
    attend_out,
    second_gain,
    second_lift,
    second_drop,
    cotangent,
):
    place = Place()
    model = hidden_in.shape[-1]
    share = hidden_in.shape[1] // 2
    own_rows = place.core * share
    hidden = lax.dynamic_slice_in_dim(hidden_in[0], own_rows, share).astype(f32)
    signal = lax.dynamic_slice_in_dim(cotangent[0], own_rows, share).astype(f32)
    order = lax.dynamic_slice_in_dim(positions[0], own_rows, share)
    order = in_order(place, gather_flat(order[:, None]))[..., 0]
    gain_rows = mixer_gain.shape[0]
    gains = jnp.stack([mixer_gain, first_gain, attend_gain, second_gain]).astype(f32)
    gains = grid_total(
        lax.dynamic_update_slice_in_dim(jnp.zeros((4, model), f32), gains, place.rank * gain_rows, 1)
    )
    query_gain, key_gain = query_scale.astype(f32), key_scale.astype(f32)
    channels = mixer_taps.shape[1] // 4
    taps = lax.dynamic_slice_in_dim(mixer_taps, place.seat * channels, channels, 1).astype(f32)

    mixer_weights = spread_weights(place, pack_mixer(mixer_in, mixer_out))
    first_weights = spread_weights(place, pack_forward(first_lift, first_drop))
    attend_weights = spread_weights(place, pack_attend(query_weight, pair_weight, attend_out))
    second_weights = spread_weights(place, pack_forward(second_lift, second_drop))

    hidden, mixer_stored = mixer_forward(place, hidden, order, gains[0], mixer_weights, taps)
    hidden, first_stored = feed_forward(hidden, gains[1], first_weights)
    hidden, attend_stored = attend_forward(
        place, hidden, order, gains[2], attend_weights, query_gain, key_gain
    )
    hidden, second_stored = feed_forward(hidden, gains[3], second_weights)

    back, second_gain_term, second_term = feed_backward(signal, second_stored, gains[3], second_weights)
    second_total = collect_gradient(place, second_term)
    back, attend_gain_term, attend_term, scale_terms = attend_backward(
        place, back, attend_stored, gains[2], attend_weights, query_gain, key_gain
    )
    attend_total = collect_gradient(place, attend_term)
    back, first_gain_term, first_term = feed_backward(back, first_stored, gains[1], first_weights)
    first_total = collect_gradient(place, first_term)
    back, mixer_gain_term, mixer_term, tap_term = mixer_backward(
        place, back, mixer_stored, gains[0], mixer_weights, taps
    )
    mixer_total = collect_gradient(place, mixer_term)

    small = jnp.concatenate(
        [mixer_gain_term, first_gain_term, attend_gain_term, second_gain_term, scale_terms[0], scale_terms[1]]
    )
    small = small + swap_core(small)
    tap_full = lax.dynamic_update_slice_in_dim(
        jnp.zeros((3, mixer_taps.shape[1]), f32), tap_term, place.seat * channels, 1
    )
    small = grid_total(jnp.concatenate([small, tap_full.reshape(-1)]))
    gain_totals = lax.dynamic_slice_in_dim(
        small[: 4 * model].reshape(4, model), place.rank * gain_rows, gain_rows, 1
    )
    scale_totals = small[4 * model : 4 * model + 2 * HD].reshape(2, HD)
    tap_total = small[4 * model + 2 * HD :].reshape(tap_full.shape)

    def both_cores(own):
        return flip_if(place.core, jnp.stack([own, swap_core(own)]), 0).reshape(1, 2 * share, model)

    rows = mixer_in.shape[0]
    in_columns = 3 * channels
    inner = attend_total.shape[-1] - query_weight.shape[1] // 4
    queries = query_weight.shape[1] // 4
    return (
        both_cores(hidden.astype(bf16)),
        both_cores(back),
        gain_totals[0],
        all_seats(mixer_total[..., :in_columns].reshape(4, rows, 3, channels)),
        tap_total,
        all_seats(mixer_total[..., in_columns:]),
        gain_totals[1],
        all_seats(first_total[:, :2].transpose(0, 2, 1, 3)),
        all_seats(first_total[:, 2]),
        gain_totals[2],
        all_seats(attend_total[..., :queries]),
        all_seats(attend_total[..., queries:inner].reshape(4, rows, 2, -1)),
        scale_totals[0],
        scale_totals[1],
        all_seats(attend_total[..., inner:]),
        gain_totals[3],
        all_seats(second_total[:, :2].transpose(0, 2, 1, 3)),
        all_seats(second_total[:, 2]),
    )


def solution(mesh):
    grid = ("dp", "seq")
    return jax.shard_map(
        body,
        mesh=mesh,
        in_specs=(
            P("dp", "seq", None),
            P("dp", "seq"),
            P(grid),
            P(grid, None, "mp"),
            P(None, "mp"),
            P(grid, "mp"),
            P(grid),
            P(grid, None, "mp"),
            P(grid, "mp"),
            P(grid),
            P(grid, "mp"),
            P(grid, None, "mp"),
            P(),
            P(),
            P(grid, "mp"),
            P(grid),
            P(grid, None, "mp"),
            P(grid, "mp"),
            P("dp", "seq", None),
        ),
        out_specs=(
            P("dp", "seq", None),
            P("dp", "seq", None),
            P(grid),
            P(grid, None, "mp"),
            P(None, "mp"),
            P(grid, "mp"),
            P(grid),
            P(grid, None, "mp"),
            P(grid, "mp"),
            P(grid),
            P(grid, "mp"),
            P(grid, None, "mp"),
            P(),
            P(),
            P(grid, "mp"),
            P(grid),
            P(grid, None, "mp"),
            P(grid, "mp"),
        ),
        check_vma=False,
    )
```

```python
import jax
import jax.numpy as jnp
from jax import lax
from jax.sharding import PartitionSpec as P

HD = 64
FIRST_AXIS, SECOND_AXIS = "dp", "dp"

epsilon = 1e-05
rope_base = 1000000.0
bf16 = jnp.bfloat16
f32 = jnp.float32


def rms_scale(values):
    return lax.rsqrt(jnp.mean(values * values, axis=-1, keepdims=True) + epsilon)


def norm_back(back_normed, normed, inverse):
    return inverse * (back_normed - normed * jnp.mean(back_normed * normed, axis=-1, keepdims=True))


def frequencies():
    exponent = jnp.arange(HD // 2, dtype=f32) * (2.0 / HD)
    return jnp.power(rope_base, -exponent)


def rotate(values, cosines, sine_table):
    middle = values.shape[-1] // 2
    leading = values[..., :middle]
    trailing = values[..., middle:]
    return jnp.concatenate(
        [leading * cosines - trailing * sine_table, trailing * cosines + leading * sine_table],
        axis=-1,
    )


def dot(pattern, first, second):
    return jnp.einsum(pattern, first, second, preferred_element_type=f32)


class Team:
    def __init__(self, axis):
        self.axis = axis
        self.across = "seq" if axis == "dp" else "dp"
        self.size = lax.axis_size(axis)
        self.seat = lax.axis_index(axis)


def swap(array, axis, mask):
    return lax.ppermute(array, axis, [(i, i ^ mask) for i in range(lax.axis_size(axis))])


def swap_core(array):
    return swap(array, "mp", 1)


def shift(array, by):
    count = lax.axis_size("seq")
    return lax.ppermute(array, "seq", [(i, i + by) for i in range(count) if 0 <= i + by < count])


def zero(token):
    element = token[(0,) * token.ndim].astype(f32)
    return (element * 0.0).astype(jnp.int32)


def take(array, index, axis):
    return lax.dynamic_index_in_dim(array, index, axis, keepdims=False)


def gather_tokens(team, own):
    mine = jnp.concatenate([own] + [swap(own, team.axis, mask) for mask in range(1, team.size)], axis=0)
    return mine, swap_core(mine)


def scatter_tokens(team, mine, other):
    received = swap_core(other.astype(bf16)).astype(f32)
    rows = mine.shape[0] // team.size
    both = mine + received
    total = both[:rows]
    sends = [(mask, both[mask * rows : (mask + 1) * rows].astype(bf16)) for mask in range(team.size - 1, 0, -1)]
    for mask, send in sends:
        total = total + swap(send, team.axis, mask).astype(f32)
    return total, sends[-1][1]


def true_order(core, sequences, halves):
    mine, other = (half.reshape(sequences, -1, half.shape[-1]) for half in halves)
    return jnp.where(
        core == 0, jnp.concatenate([mine, other], axis=1), jnp.concatenate([other, mine], axis=1)
    )


def own_halves(core, ordered):
    rows = ordered.shape[1] // 2
    return [
        lax.dynamic_slice_in_dim(ordered, at * rows, rows, 1).reshape(-1, ordered.shape[-1])
        for at in (core, 1 - core)
    ]


def team_rows(team, piece_of):
    return [
        swap(piece_of(team.seat ^ mask), team.axis, mask) if mask else piece_of(team.seat)
        for mask in range(team.size)
    ]


def all_rows(team, pieces, late=0):
    lead, (rows, columns) = pieces[0].shape[:-2], pieces[0].shape[-2:]
    plain = (0,) * len(lead)
    near = jnp.zeros(lead + (team.size, rows, columns), pieces[0].dtype)
    for mask, piece in enumerate(pieces):
        near = lax.dynamic_update_slice(
            near, jnp.expand_dims(piece, len(lead)), plain + ((team.seat ^ mask) + late, 0, 0)
        )
    if team.axis == "dp":
        whole = lax.all_gather(near, team.across, axis=len(lead) + 1, tiled=True)
    else:
        near = near.reshape(lead + (team.size * rows, columns))
        whole = lax.all_gather(near, team.across, axis=len(lead), tiled=True)
    return whole.reshape(lead + (-1, columns))


def summed_rows(team, gradient):
    columns = gradient.shape[-1]
    teams = lax.axis_size(team.across)
    if team.axis == "dp":
        split = gradient.reshape(team.size, teams, -1, columns).swapaxes(0, 1)
    else:
        split = gradient.reshape(teams, team.size, -1, columns)
    rows = split.shape[2]
    part = lax.psum_scatter(split.reshape(-1, columns), team.across, scatter_dimension=0, tiled=True)
    return part.reshape(team.size, rows, columns)


def every_seat(team, part, late=0):
    axis = part.ndim - 3
    pieces = []
    for mask in range(team.size):
        piece = take(part, (team.seat ^ mask) + late, axis)
        pieces.append(swap(piece, team.axis, mask) if mask else piece)
    seats = jnp.stack(pieces)
    shape, bits = seats.shape, team.size.bit_length() - 1
    seats = seats.reshape((2,) * bits + shape[1:])
    for bit in range(bits):
        seats = jnp.where((team.seat >> bit) & 1 == 1, jnp.flip(seats, bits - 1 - bit), seats)
    return seats.reshape(shape).astype(f32)


def hidden_width(units, seats):
    tiles = -(-units // (128 * seats))
    return tiles * 128 if units % 128 == 0 else units // seats


def hidden_start(units, seats, seat):
    width = hidden_width(units, seats)
    return jnp.minimum(seat * width, units - width)


def hidden_mask(units, seats, seat):
    width = hidden_width(units, seats)
    doubled = seat * width - hidden_start(units, seats, seat)
    return (lax.broadcasted_iota(jnp.int32, (1, width), 1) >= doubled).astype(f32)


def joined_hidden(units, pieces):
    seats = len(pieces)
    width = hidden_width(units, seats)
    parts = []
    for seat in range(seats):
        low, start = seat * width, min(seat * width, units - width)
        if low < units:
            parts.append(pieces[seat][..., low - start : min(low + width, units) - start])
    return jnp.concatenate(parts, axis=-1)


def quarter(array, seat):
    width = array.shape[-1] // 4
    return array[..., seat * width : (seat + 1) * width]


def all_seats(array):
    return jnp.concatenate([array[i] for i in range(4)], axis=-1)


def pack_mixer(weight_in, weight_out):
    seats = [
        jnp.concatenate([quarter(weight_in[:, k], i) for k in range(3)] + [quarter(weight_out, i)], axis=-1)
        for i in range(4)
    ]
    return jnp.stack(seats)


def pack_attend(query_weight, pair_weight, out_weight):
    seats = [
        jnp.concatenate(
            [quarter(query_weight, i)]
            + [quarter(pair_weight[:, k], i) for k in range(2)]
            + [quarter(out_weight, i)],
            axis=-1,
        )
        for i in range(4)
    ]
    return jnp.stack(seats)


def lowered_norm(hidden, gain):
    inverse = rms_scale(hidden)
    normed = hidden * inverse
    return inverse, normed, (normed * gain).astype(bf16)


def after_norm(back_out, back_normed, normed, inverse, gain):
    gain_term = jnp.sum(back_normed * normed, axis=0)
    return back_out + norm_back(back_normed * gain, normed, inverse), gain_term


def project(pattern, halves, weights):
    return [dot(pattern, half, weights) for half in halves]


def project_out(team, pattern, halves, weights):
    other = dot(pattern, halves[1], weights)
    mine = dot(pattern, halves[0], weights)
    return scatter_tokens(team, mine, other)


def outer(first, second):
    return (dot("td,tf->df", first[0], second[0]) + dot("td,tf->df", first[1], second[1])).astype(bf16)


def feed_active(tokens, lift, mask):
    gate = dot("td,df->tf", tokens, lift[0])
    up = dot("td,df->tf", tokens, lift[1])
    return gate, up, (jax.nn.silu(gate) * up * mask).astype(bf16)


def feed_back(back_tokens, gate, up, drop, mask):
    back_active = dot("td,df->tf", back_tokens, drop) * mask
    sigmoid_value = jax.nn.sigmoid(gate)
    back_gate = back_active * up * sigmoid_value * (1.0 + gate * (1.0 - sigmoid_value))
    return back_gate.astype(bf16), (back_active * gate * sigmoid_value).astype(bf16)


def feed_forward(team, hidden, gain, lift, mask):
    inverse, normed, lowered = lowered_norm(hidden, gain)
    tokens = gather_tokens(team, lowered)
    gate, up, active = zip(*[feed_active(half, lift, mask) for half in tokens])
    return inverse, normed, tokens, gate, up, active


def feed_backward(team, back_out, back_tokens, stored, gain, lift, drop, mask):
    inverse, normed, tokens, gate, up, active = stored
    back_gate, back_up = zip(
        *[feed_back(back_tokens[i], gate[i], up[i], drop, mask) for i in range(2)]
    )
    terms = [
        dot("tf,df->td", back_gate[i], lift[0]) + dot("tf,df->td", back_up[i], lift[1]) for i in (1, 0)
    ]
    back_normed, sent = scatter_tokens(team, terms[1], terms[0])
    drop_term = outer(back_tokens, active)
    lift_terms = [outer(tokens, back_gate), outer(tokens, back_up)]
    back_hidden, gain_term = after_norm(back_out, back_normed, normed, inverse, gain)
    return back_hidden, gain_term, lift_terms + [drop_term]


def mixer_forward(team, core, hidden, token_halves, order, gain, weights, taps):
    inverse = rms_scale(hidden)
    normed = hidden * inverse
    tokens = [lowered_norm(half.astype(f32), gain)[2] for half in token_halves]
    channels = taps.shape[1]
    parts = true_order(core, team.size, project("td,dc->tc", tokens, weights[:, : 3 * channels]))
    gate_in, gate_out, value = (parts[..., i * channels : (i + 1) * channels] for i in range(3))
    mixed = (gate_in * value).astype(bf16)
    earlier = shift(mixed[:, -2:], 1)
    padded = jnp.concatenate([earlier, mixed], axis=1).astype(f32)
    one_back = (order >= 1).astype(f32)[..., None]
    two_back = (order >= 2).astype(f32)[..., None]
    convolved = (
        taps[2] * padded[:, 2:] + taps[1] * padded[:, 1:-1] * one_back + taps[0] * padded[:, :-2] * two_back
    )
    gated = own_halves(core, (gate_out * convolved).astype(bf16))
    out, sent = project_out(team, "tc,dc->td", gated, weights[:, 3 * channels :])
    stored = (inverse, normed, tokens, gate_in, gate_out, value, padded, convolved, gated, one_back, two_back)
    return hidden + out, stored, parts


def mixer_backward(team, core, back_out, stored, gain, weights, taps):
    inverse, normed, tokens, gate_in, gate_out, value, padded, convolved, gated, one_back, two_back = stored
    channels = taps.shape[1]
    back_tokens = gather_tokens(team, back_out.astype(bf16))
    back_gated = true_order(core, team.size, project("td,dc->tc", back_tokens, weights[:, 3 * channels :]))
    back_conv = back_gated * gate_out
    back_padded = (
        jnp.pad(taps[2] * back_conv, ((0, 0), (2, 0), (0, 0)))
        + jnp.pad(taps[1] * back_conv * one_back, ((0, 0), (1, 1), (0, 0)))
        + jnp.pad(taps[0] * back_conv * two_back, ((0, 0), (0, 2), (0, 0)))
    )
    later = shift(back_padded[:, :2], -1)
    back_mixed = back_padded[:, 2:] + jnp.pad(later, ((0, 0), (back_conv.shape[1] - 2, 0), (0, 0)))
    back_parts = own_halves(
        core,
        jnp.concatenate(
            [back_mixed * value, back_gated * convolved, back_mixed * gate_in], axis=-1
        ).astype(bf16),
    )
    back_normed, sent = project_out(team, "tc,dc->td", back_parts, weights[:, : 3 * channels])
    tap_term = jnp.stack(
        [
            jnp.sum(back_conv * padded[:, :-2] * two_back, axis=(0, 1)),
            jnp.sum(back_conv * padded[:, 1:-1] * one_back, axis=(0, 1)),
            jnp.sum(back_conv * padded[:, 2:], axis=(0, 1)),
        ]
    )
    term = jnp.concatenate([outer(tokens, back_parts), outer(back_tokens, gated)], axis=-1)
    back_hidden, gain_term = after_norm(back_out, back_normed, normed, inverse, gain)
    return back_hidden, gain_term, term, tap_term, back_gated


def attend_forward(team, core, hidden, order, gain, weights, query_gain, key_gain):
    inverse, normed, lowered = lowered_norm(hidden, gain)
    tokens = gather_tokens(team, lowered)
    heads = weights.shape[1] * 3 // 8 // HD
    groups = weights.shape[1] // 8 // HD
    repeat = heads // groups
    inner = (heads + 2 * groups) * HD
    mixed = true_order(core, team.size, project("td,dc->tc", tokens, weights[:, :inner]))
    sequences, count = mixed.shape[:2]
    query_heads = mixed[..., : heads * HD].reshape(sequences, count, heads, HD)
    key_heads = mixed[..., heads * HD : (heads + groups) * HD].reshape(sequences, count, groups, HD)
    value_low = mixed[..., (heads + groups) * HD :].astype(bf16)
    angles = order.astype(f32)[..., None] * frequencies()
    cosines, sines = jnp.cos(angles)[:, :, None, :], jnp.sin(angles)[:, :, None, :]
    query_inverse = rms_scale(query_heads)
    query_normed = query_heads * query_inverse
    query_rot = rotate(query_normed * query_gain, cosines, sines).astype(bf16)
    key_inverse = rms_scale(key_heads)
    key_normed = key_heads * key_inverse
    key_rot = rotate(key_normed * key_gain, cosines, sines).astype(bf16)
    pair = jnp.concatenate([key_rot.reshape(sequences, count, groups * HD), value_low], axis=-1)
    blocks = lax.axis_size("seq")
    here = lax.axis_index("seq")
    slots = jnp.concatenate([shift(pair, i) if i else pair for i in range(blocks)], axis=1)
    keys = slots[..., : groups * HD].reshape(sequences, -1, groups, HD)
    values = slots[..., groups * HD :].reshape(sequences, -1, groups, HD)
    grouped = query_rot.reshape(sequences, count, groups, repeat, HD)
    row_index = here * count + jnp.arange(count, dtype=jnp.int32)
    row_first = row_index[None] - order
    key_index = jnp.concatenate(
        [(here - i) * count + jnp.arange(count, dtype=jnp.int32) for i in range(blocks)]
    )
    allowed = (key_index[None, None, :] <= row_index[None, :, None]) & (
        key_index[None, None, :] >= row_first[:, :, None]
    )
    scores = dot("vqgrd,vkgd->vgrqk", grouped, keys) * HD**-0.5
    scores = jnp.where(allowed[:, None, None], scores, -1e30)
    probs = jnp.exp(scores - jnp.max(scores, axis=-1, keepdims=True))
    probs = probs / jnp.sum(probs, axis=-1, keepdims=True)
    attended = dot("vgrqk,vkgd->vqgrd", probs.astype(bf16), values).astype(bf16)
    attended = own_halves(core, attended.reshape(sequences, count, heads * HD))
    out, sent = project_out(team, "tc,dc->td", attended, weights[:, inner:])
    stored = (
        inverse,
        normed,
        tokens,
        query_inverse,
        query_normed,
        key_inverse,
        key_normed,
        cosines,
        sines,
        grouped,
        keys,
        values,
        probs,
        attended,
    )
    return hidden + out, stored, mixed


def attend_backward(team, core, back_out, stored, gain, weights, query_gain, key_gain):
    (
        inverse,
        normed,
        tokens,
        query_inverse,
        query_normed,
        key_inverse,
        key_normed,
        cosines,
        sines,
        grouped,
        keys,
        values,
        probs,
        attended,
    ) = stored
    sequences, count, groups, repeat = grouped.shape[:4]
    heads = groups * repeat
    inner = (heads + 2 * groups) * HD
    back_tokens = gather_tokens(team, back_out.astype(bf16))
    back_attended = true_order(core, team.size, project("td,dc->tc", back_tokens, weights[:, inner:])).astype(bf16)
    back_grouped = back_attended.reshape(sequences, count, groups, repeat, HD)
    back_probs = dot("vqgrd,vkgd->vgrqk", back_grouped, values)
    row_dot = jnp.sum(probs * back_probs, axis=-1, keepdims=True)
    back_scores = (probs * (back_probs - row_dot)).astype(bf16)
    back_query_rot = dot("vgrqk,vkgd->vqgrd", back_scores, keys) * HD**-0.5
    back_keys = dot("vgrqk,vqgrd->vkgd", back_scores, grouped) * HD**-0.5
    back_values = dot("vgrqk,vqgrd->vkgd", probs.astype(bf16), back_grouped)
    back_slots = jnp.concatenate(
        [
            back_keys.reshape(sequences, -1, count, groups * HD),
            back_values.reshape(sequences, -1, count, groups * HD),
        ],
        axis=-1,
    )
    back_pair = back_slots[:, 0]
    for i in range(1, back_slots.shape[1]):
        back_pair = back_pair + shift(back_slots[:, i].astype(bf16), -i).astype(f32)
    back_query_scaled = rotate(back_query_rot.reshape(sequences, count, heads, HD), cosines, -sines)
    query_scale_term = jnp.sum(back_query_scaled * query_normed, axis=(0, 1, 2))
    back_query = norm_back(back_query_scaled * query_gain, query_normed, query_inverse)
    back_key_rot = back_pair[..., : groups * HD].reshape(sequences, count, groups, HD)
    back_key_scaled = rotate(back_key_rot, cosines, -sines)
    key_scale_term = jnp.sum(back_key_scaled * key_normed, axis=(0, 1, 2))
    back_key = norm_back(back_key_scaled * key_gain, key_normed, key_inverse)
    back_mixed = jnp.concatenate(
        [
            back_query.reshape(sequences, count, heads * HD),
            back_key.reshape(sequences, count, groups * HD),
            back_pair[..., groups * HD :],
        ],
        axis=-1,
    ).astype(bf16)
    back_mixed = own_halves(core, back_mixed)
    back_normed, sent = project_out(team, "tc,dc->td", back_mixed, weights[:, :inner])
    term = jnp.concatenate([outer(tokens, back_mixed), outer(back_tokens, attended)], axis=-1)
    back_hidden, gain_term = after_norm(back_out, back_normed, normed, inverse, gain)
    return back_hidden, gain_term, term, (query_scale_term, key_scale_term), back_attended


def grid_total(array):
    for axis in ("dp", "seq"):
        mask = 1
        while mask < lax.axis_size(axis):
            array = array + swap(array, axis, mask)
            mask *= 2
    return array


def body(
    hidden_in,
    positions,
    mixer_gain,
    mixer_in,
    mixer_taps,
    mixer_out,
    first_gain,
    first_lift,
    first_drop,
    attend_gain,
    query_weight,
    pair_weight,
    query_scale,
    key_scale,
    attend_out,
    second_gain,
    second_lift,
    second_drop,
    cotangent,
):
    core = lax.axis_index("mp")
    team = Team("dp")
    first_team, second_team = Team(FIRST_AXIS), Team(SECOND_AXIS)
    rank = lax.axis_index("dp") * lax.axis_size("seq") + lax.axis_index("seq")
    model = hidden_in.shape[-1]
    share = hidden_in.shape[1] // 2
    own_tokens = lax.dynamic_slice_in_dim(hidden_in[0], core * share, share)
    hidden = own_tokens.astype(f32)
    signal_low = lax.dynamic_slice_in_dim(cotangent[0], core * share, share)
    signal = signal_low.astype(f32)
    query_gain, key_gain = query_scale.astype(f32), key_scale.astype(f32)
    channels = mixer_taps.shape[1] // team.size
    taps = lax.dynamic_slice_in_dim(mixer_taps, team.seat * channels, channels, 1).astype(f32)
    units = first_drop.shape[1]
    first_mask = hidden_mask(units, first_team.size, first_team.seat)
    second_mask = hidden_mask(units, second_team.size, second_team.seat)

    def feed_piece(on, lift, drop, late):
        both = jnp.concatenate([lift.transpose(1, 0, 2), drop[None]], axis=0)
        width = hidden_width(units, on.size)
        return lambda seat: lax.dynamic_slice_in_dim(both, hidden_start(units, on.size, seat) + late, width, 2)

    token_halves = gather_tokens(team, own_tokens)
    packed = pack_mixer(mixer_in, mixer_out)
    got = team_rows(team, lambda seat: take(packed, seat, 0))
    mixer_weights = all_rows(team, got)
    near_done = zero(got[-1])

    got_first = team_rows(first_team, feed_piece(first_team, first_lift, first_drop, near_done))
    first_lift_all = all_rows(first_team, [piece[:2] for piece in got_first])
    first_drop_all = all_rows(first_team, [piece[2] for piece in got_first])
    near_done = zero(got_first[-1])

    gain_rows = mixer_gain.shape[0]
    gains = jnp.stack([mixer_gain, first_gain, attend_gain, second_gain]).astype(f32)
    gains = grid_total(
        lax.dynamic_update_slice_in_dim(jnp.zeros((4, model), f32), gains, rank * gain_rows + near_done, 1)
    )
    own_places = positions[0] + near_done
    order = jnp.stack([own_places] + [swap(own_places, team.axis, mask) for mask in range(1, team.size)])

    packed_attend = pack_attend(query_weight, pair_weight, attend_out)
    got_attend = team_rows(team, lambda seat: take(packed_attend, seat + near_done, 0))
    got_second = team_rows(second_team, feed_piece(second_team, second_lift, second_drop, near_done))

    after_mixer, mixer_stored, parts = mixer_forward(
        team, core, hidden, token_halves, order, gains[0], mixer_weights, taps
    )
    mixed_done = zero(parts)
    attend_weights = all_rows(team, got_attend, mixed_done)
    second_lift_all = all_rows(second_team, [piece[:2] for piece in got_second], mixed_done)
    second_drop_all = all_rows(second_team, [piece[2] for piece in got_second], mixed_done)

    first_stored = feed_forward(first_team, after_mixer, gains[1], first_lift_all, first_mask)
    out, sent = project_out(first_team, "tf,df->td", first_stored[-1], first_drop_all)
    after_first = after_mixer + out
    after_attend, attend_stored, mixed = attend_forward(
        team, core, after_first, order, gains[2], attend_weights, query_gain, key_gain
    )
    signal_low = signal_low + zero(mixed).astype(bf16)
    signal_tokens = gather_tokens(second_team, signal_low)
    second_stored = feed_forward(second_team, after_attend, gains[3], second_lift_all, second_mask)

    back, second_gain_term, second_terms = feed_backward(
        second_team, signal, signal_tokens, second_stored, gains[3], second_lift_all, second_drop_all, second_mask
    )
    second_part = [summed_rows(second_team, term) for term in second_terms]
    back, attend_gain_term, attend_term, scale_terms, back_attended = attend_backward(
        team, core, back, attend_stored, gains[2], attend_weights, query_gain, key_gain
    )
    attend_part = summed_rows(team, attend_term)
    late = zero(back_attended).astype(bf16)
    out, sent = project_out(second_team, "tf,df->td", [half + late for half in second_stored[-1]], second_drop_all)
    result = after_attend + out

    first_back_tokens = gather_tokens(first_team, back.astype(bf16))
    back, first_gain_term, first_terms = feed_backward(
        first_team, back, first_back_tokens, first_stored, gains[1], first_lift_all, first_drop_all, first_mask
    )
    first_part = [summed_rows(first_team, term) for term in first_terms]
    back, mixer_gain_term, mixer_term, tap_term, back_gated = mixer_backward(
        team, core, back, mixer_stored, gains[0], mixer_weights, taps
    )
    mixer_part = summed_rows(team, mixer_term)
    gated_done = zero(back_gated)
    second_total = every_seat(second_team, jnp.stack(second_part), gated_done)
    attend_total = every_seat(team, attend_part, gated_done)
    first_total = every_seat(first_team, jnp.stack(first_part))
    mixer_total = every_seat(team, mixer_part)

    small = jnp.concatenate(
        [mixer_gain_term, first_gain_term, attend_gain_term, second_gain_term, scale_terms[0], scale_terms[1]]
    )
    small = small + swap_core(small)
    tap_full = lax.dynamic_update_slice_in_dim(
        jnp.zeros((3, mixer_taps.shape[1]), f32), tap_term, team.seat * channels, 1
    )
    small = grid_total(jnp.concatenate([small, tap_full.reshape(-1)]))
    gain_totals = lax.dynamic_slice_in_dim(
        small[: 4 * model].reshape(4, model), rank * gain_rows, gain_rows, 1
    )
    scale_totals = small[4 * model : 4 * model + 2 * HD].reshape(2, HD)
    tap_total = small[4 * model + 2 * HD :].reshape(tap_full.shape)

    def both_cores(own):
        return true_order(core, 1, [own, swap_core(own)])

    rows = mixer_in.shape[0]
    in_columns = 3 * channels
    inner = attend_total.shape[-1] - query_weight.shape[1] // 4
    queries = query_weight.shape[1] // 4
    return (
        both_cores(result.astype(bf16)),
        both_cores(back),
        gain_totals[0],
        all_seats(mixer_total[..., :in_columns].reshape(4, rows, 3, channels)),
        tap_total,
        all_seats(mixer_total[..., in_columns:]),
        gain_totals[1],
        joined_hidden(units, first_total[:, :2]).transpose(1, 0, 2),
        joined_hidden(units, first_total[:, 2]),
        gain_totals[2],
        all_seats(attend_total[..., :queries]),
        all_seats(attend_total[..., queries:inner].reshape(4, rows, 2, -1)),
        scale_totals[0],
        scale_totals[1],
        all_seats(attend_total[..., inner:]),
        gain_totals[3],
        joined_hidden(units, second_total[:, :2]).transpose(1, 0, 2),
        joined_hidden(units, second_total[:, 2]),
    )


def solution(mesh):
    grid = ("dp", "seq")
    return jax.shard_map(
        body,
        mesh=mesh,
        in_specs=(
            P("dp", "seq", None),
            P("dp", "seq"),
            P(grid),
            P(grid, None, "mp"),
            P(None, "mp"),
            P(grid, "mp"),
            P(grid),
            P(grid, None, "mp"),
            P(grid, "mp"),
            P(grid),
            P(grid, "mp"),
            P(grid, None, "mp"),
            P(),
            P(),
            P(grid, "mp"),
            P(grid),
            P(grid, None, "mp"),
            P(grid, "mp"),
            P("dp", "seq", None),
        ),
        out_specs=(
            P("dp", "seq", None),
            P("dp", "seq", None),
            P(grid),
            P(grid, None, "mp"),
            P(None, "mp"),
            P(grid, "mp"),
            P(grid),
            P(grid, None, "mp"),
            P(grid, "mp"),
            P(grid),
            P(grid, "mp"),
            P(grid, None, "mp"),
            P(),
            P(),
            P(grid, "mp"),
            P(grid),
            P(grid, None, "mp"),
            P(grid, "mp"),
        ),
        check_vma=False,
    )
```

```python
import jax
import jax.numpy as jnp
from jax import lax
from jax.sharding import PartitionSpec as P

HD = 64
FIRST_AXIS, SECOND_AXIS = "dp", "dp"

epsilon = 1e-05
rope_base = 1000000.0
bf16 = jnp.bfloat16
f32 = jnp.float32


def rms_scale(values):
    return lax.rsqrt(jnp.mean(values * values, axis=-1, keepdims=True) + epsilon)


def norm_back(back_normed, normed, inverse):
    return inverse * (back_normed - normed * jnp.mean(back_normed * normed, axis=-1, keepdims=True))


def frequencies():
    exponent = jnp.arange(HD // 2, dtype=f32) * (2.0 / HD)
    return jnp.power(rope_base, -exponent)


def rotate(values, cosines, sine_table):
    middle = values.shape[-1] // 2
    leading = values[..., :middle]
    trailing = values[..., middle:]
    return jnp.concatenate(
        [leading * cosines - trailing * sine_table, trailing * cosines + leading * sine_table],
        axis=-1,
    )


def dot(pattern, first, second):
    return jnp.einsum(pattern, first, second, preferred_element_type=f32)


class Team:
    def __init__(self, axis):
        self.axis = axis
        self.across = "seq" if axis == "dp" else "dp"
        self.size = lax.axis_size(axis)
        self.seat = lax.axis_index(axis)


def swap(array, axis, mask):
    return lax.ppermute(array, axis, [(i, i ^ mask) for i in range(lax.axis_size(axis))])


def swap_core(array):
    return swap(array, "mp", 1)


def shift(array, by):
    count = lax.axis_size("seq")
    return lax.ppermute(array, "seq", [(i, i + by) for i in range(count) if 0 <= i + by < count])


def zero(token):
    element = token[(0,) * token.ndim].astype(f32)
    return (element * 0.0).astype(jnp.int32)


def take(array, index, axis):
    return lax.dynamic_index_in_dim(array, index, axis, keepdims=False)


def gather_tokens(team, own):
    mine = jnp.concatenate([own] + [swap(own, team.axis, mask) for mask in range(1, team.size)], axis=0)
    return mine, swap_core(mine)


def scatter_tokens(team, mine, other):
    received = swap_core(other.astype(bf16)).astype(f32)
    rows = mine.shape[0] // team.size
    both = mine + received
    total = both[:rows]
    sends = [(mask, both[mask * rows : (mask + 1) * rows].astype(bf16)) for mask in range(team.size - 1, 0, -1)]
    for mask, send in sends:
        total = total + swap(send, team.axis, mask).astype(f32)
    return total, sends[-1][1]


def true_order(core, sequences, halves):
    mine, other = (half.reshape(sequences, -1, half.shape[-1]) for half in halves)
    return jnp.where(
        core == 0, jnp.concatenate([mine, other], axis=1), jnp.concatenate([other, mine], axis=1)
    )


def own_halves(core, ordered):
    rows = ordered.shape[1] // 2
    return [
        lax.dynamic_slice_in_dim(ordered, at * rows, rows, 1).reshape(-1, ordered.shape[-1])
        for at in (core, 1 - core)
    ]


def team_rows(team, piece_of):
    return [
        swap(piece_of(team.seat ^ mask), team.axis, mask) if mask else piece_of(team.seat)
        for mask in range(team.size)
    ]


def all_rows(team, pieces, late=0):
    lead, (rows, columns) = pieces[0].shape[:-2], pieces[0].shape[-2:]
    plain = (0,) * len(lead)
    near = jnp.zeros(lead + (team.size, rows, columns), pieces[0].dtype)
    for mask, piece in enumerate(pieces):
        near = lax.dynamic_update_slice(
            near, jnp.expand_dims(piece, len(lead)), plain + ((team.seat ^ mask) + late, 0, 0)
        )
    if team.axis == "dp":
        whole = lax.all_gather(near, team.across, axis=len(lead) + 1, tiled=True)
    else:
        near = near.reshape(lead + (team.size * rows, columns))
        whole = lax.all_gather(near, team.across, axis=len(lead), tiled=True)
    return whole.reshape(lead + (-1, columns))


def summed_rows(team, gradient):
    columns = gradient.shape[-1]
    teams = lax.axis_size(team.across)
    if team.axis == "dp":
        split = gradient.reshape(team.size, teams, -1, columns).swapaxes(0, 1)
    else:
        split = gradient.reshape(teams, team.size, -1, columns)
    rows = split.shape[2]
    part = lax.psum_scatter(split.reshape(-1, columns), team.across, scatter_dimension=0, tiled=True)
    return part.reshape(team.size, rows, columns)


def every_seat(team, part, late=0):
    axis = part.ndim - 3
    pieces = []
    for mask in range(team.size):
        piece = take(part, (team.seat ^ mask) + late, axis)
        pieces.append(swap(piece, team.axis, mask) if mask else piece)
    seats = jnp.stack(pieces)
    shape, bits = seats.shape, team.size.bit_length() - 1
    seats = seats.reshape((2,) * bits + shape[1:])
    for bit in range(bits):
        seats = jnp.where((team.seat >> bit) & 1 == 1, jnp.flip(seats, bits - 1 - bit), seats)
    return seats.reshape(shape).astype(f32)


def hidden_width(units, seats):
    tiles = -(-units // (128 * seats))
    return tiles * 128 if units % 128 == 0 else units // seats


def hidden_start(units, seats, seat):
    width = hidden_width(units, seats)
    return jnp.minimum(seat * width, units - width)


def hidden_mask(units, seats, seat):
    width = hidden_width(units, seats)
    doubled = seat * width - hidden_start(units, seats, seat)
    return (lax.broadcasted_iota(jnp.int32, (1, width), 1) >= doubled).astype(f32)


def joined_hidden(units, pieces):
    seats = len(pieces)
    width = hidden_width(units, seats)
    parts = []
    for seat in range(seats):
        low, start = seat * width, min(seat * width, units - width)
        if low < units:
            parts.append(pieces[seat][..., low - start : min(low + width, units) - start])
    return jnp.concatenate(parts, axis=-1)


def quarter(array, seat):
    width = array.shape[-1] // 4
    return array[..., seat * width : (seat + 1) * width]


def all_seats(array):
    return jnp.concatenate([array[i] for i in range(4)], axis=-1)


def pack_mixer(weight_in, weight_out):
    seats = [
        jnp.concatenate([quarter(weight_in[:, k], i) for k in range(3)] + [quarter(weight_out, i)], axis=-1)
        for i in range(4)
    ]
    return jnp.stack(seats)


def pack_attend(query_weight, pair_weight, out_weight):
    seats = [
        jnp.concatenate(
            [quarter(query_weight, i)]
            + [quarter(pair_weight[:, k], i) for k in range(2)]
            + [quarter(out_weight, i)],
            axis=-1,
        )
        for i in range(4)
    ]
    return jnp.stack(seats)


def lowered_norm(hidden, gain):
    inverse = rms_scale(hidden)
    normed = hidden * inverse
    return inverse, normed, (normed * gain).astype(bf16)


def after_norm(back_out, back_normed, normed, inverse, gain):
    gain_term = jnp.sum(back_normed * normed, axis=0)
    return back_out + norm_back(back_normed * gain, normed, inverse), gain_term


def project(pattern, halves, weights):
    return [dot(pattern, half, weights) for half in halves]


def project_out(team, pattern, halves, weights):
    other = dot(pattern, halves[1], weights)
    mine = dot(pattern, halves[0], weights)
    return scatter_tokens(team, mine, other)


def outer(first, second):
    return (dot("td,tf->df", first[0], second[0]) + dot("td,tf->df", first[1], second[1])).astype(bf16)


def feed_active(tokens, lift, mask):
    both = dot("td,df->tf", tokens, lift)
    width = both.shape[1] // 2
    gate, up = both[:, :width], both[:, width:]
    return gate, up, (jax.nn.silu(gate) * up * mask).astype(bf16)


def feed_back(back_tokens, gate, up, drop, mask):
    back_active = dot("td,df->tf", back_tokens, drop) * mask
    sigmoid_value = jax.nn.sigmoid(gate)
    back_gate = back_active * up * sigmoid_value * (1.0 + gate * (1.0 - sigmoid_value))
    return jnp.concatenate([back_gate, back_active * gate * sigmoid_value], axis=1).astype(bf16)


def feed_forward(team, hidden, gain, lift, mask):
    inverse, normed, lowered = lowered_norm(hidden, gain)
    tokens = gather_tokens(team, lowered)
    gate, up, active = zip(*[feed_active(half, lift, mask) for half in tokens])
    return inverse, normed, tokens, gate, up, active


def held(array, token):
    return array + zero(token).astype(array.dtype)


def feed_backward(team, back_out, back_tokens, stored, gain, lift, drop, mask, hold):
    inverse, normed, tokens, gate, up, active = stored
    back_pair = [feed_back(back_tokens[i], gate[i], up[i], drop, mask) for i in range(2)]
    back_normed, sent = project_out(team, "tf,df->td", back_pair, lift)
    drop_part = summed_rows(team, outer(back_tokens, active))
    lift_part = summed_rows(team, outer(tokens, back_pair))
    if hold:
        gain = held(gain, drop_part)
    back_hidden, gain_term = after_norm(back_out, back_normed, normed, inverse, gain)
    return back_hidden, gain_term, drop_part, lift_part


def mixer_forward(team, core, hidden, token_halves, order, gain, weights, taps):
    inverse = rms_scale(hidden)
    normed = hidden * inverse
    tokens = [lowered_norm(half.astype(f32), gain)[2] for half in token_halves]
    channels = taps.shape[1]
    parts = true_order(core, team.size, project("td,dc->tc", tokens, weights[:, : 3 * channels]))
    gate_in, gate_out, value = (parts[..., i * channels : (i + 1) * channels] for i in range(3))
    mixed = (gate_in * value).astype(bf16)
    earlier = shift(mixed[:, -2:], 1)
    padded = jnp.concatenate([earlier, mixed], axis=1).astype(f32)
    one_back = (order >= 1).astype(f32)[..., None]
    two_back = (order >= 2).astype(f32)[..., None]
    convolved = (
        taps[2] * padded[:, 2:] + taps[1] * padded[:, 1:-1] * one_back + taps[0] * padded[:, :-2] * two_back
    )
    gated = own_halves(core, (gate_out * convolved).astype(bf16))
    out, sent = project_out(team, "tc,dc->td", gated, weights[:, 3 * channels :])
    stored = (inverse, normed, tokens, gate_in, gate_out, value, padded, convolved, gated, one_back, two_back)
    return hidden + out, stored, parts


def mixer_backward(team, core, back_out, stored, gain, weights, taps):
    inverse, normed, tokens, gate_in, gate_out, value, padded, convolved, gated, one_back, two_back = stored
    channels = taps.shape[1]
    back_tokens = gather_tokens(team, back_out.astype(bf16))
    back_gated = true_order(core, team.size, project("td,dc->tc", back_tokens, weights[:, 3 * channels :]))
    back_conv = back_gated * gate_out
    back_padded = (
        jnp.pad(taps[2] * back_conv, ((0, 0), (2, 0), (0, 0)))
        + jnp.pad(taps[1] * back_conv * one_back, ((0, 0), (1, 1), (0, 0)))
        + jnp.pad(taps[0] * back_conv * two_back, ((0, 0), (0, 2), (0, 0)))
    )
    later = shift(back_padded[:, :2], -1)
    back_mixed = back_padded[:, 2:] + jnp.pad(later, ((0, 0), (back_conv.shape[1] - 2, 0), (0, 0)))
    back_parts = own_halves(
        core,
        jnp.concatenate(
            [back_mixed * value, back_gated * convolved, back_mixed * gate_in], axis=-1
        ).astype(bf16),
    )
    back_normed, sent = project_out(team, "tc,dc->td", back_parts, weights[:, : 3 * channels])
    tap_term = jnp.stack(
        [
            jnp.sum(back_conv * padded[:, :-2] * two_back, axis=(0, 1)),
            jnp.sum(back_conv * padded[:, 1:-1] * one_back, axis=(0, 1)),
            jnp.sum(back_conv * padded[:, 2:], axis=(0, 1)),
        ]
    )
    term = jnp.concatenate([outer(tokens, back_parts), outer(back_tokens, gated)], axis=-1)
    back_hidden, gain_term = after_norm(back_out, back_normed, normed, inverse, gain)
    return back_hidden, gain_term, term, tap_term, back_gated


def attend_forward(team, core, hidden, order, gain, weights, query_gain, key_gain):
    inverse, normed, lowered = lowered_norm(hidden, gain)
    tokens = gather_tokens(team, lowered)
    heads = weights.shape[1] * 3 // 8 // HD
    groups = weights.shape[1] // 8 // HD
    repeat = heads // groups
    inner = (heads + 2 * groups) * HD
    mixed = true_order(core, team.size, project("td,dc->tc", tokens, weights[:, :inner]))
    sequences, count = mixed.shape[:2]
    query_heads = mixed[..., : heads * HD].reshape(sequences, count, heads, HD)
    key_heads = mixed[..., heads * HD : (heads + groups) * HD].reshape(sequences, count, groups, HD)
    value_low = mixed[..., (heads + groups) * HD :].astype(bf16)
    angles = order.astype(f32)[..., None] * frequencies()
    cosines, sines = jnp.cos(angles)[:, :, None, :], jnp.sin(angles)[:, :, None, :]
    query_inverse = rms_scale(query_heads)
    query_normed = query_heads * query_inverse
    query_rot = rotate(query_normed * query_gain, cosines, sines).astype(bf16)
    key_inverse = rms_scale(key_heads)
    key_normed = key_heads * key_inverse
    key_rot = rotate(key_normed * key_gain, cosines, sines).astype(bf16)
    pair = jnp.concatenate([key_rot.reshape(sequences, count, groups * HD), value_low], axis=-1)
    blocks = lax.axis_size("seq")
    here = lax.axis_index("seq")
    slots = jnp.concatenate([shift(pair, i) if i else pair for i in range(blocks)], axis=1)
    keys = slots[..., : groups * HD].reshape(sequences, -1, groups, HD)
    values = slots[..., groups * HD :].reshape(sequences, -1, groups, HD)
    grouped = query_rot.reshape(sequences, count, groups, repeat, HD)
    row_index = here * count + jnp.arange(count, dtype=jnp.int32)
    row_first = row_index[None] - order
    key_index = jnp.concatenate(
        [(here - i) * count + jnp.arange(count, dtype=jnp.int32) for i in range(blocks)]
    )
    allowed = (key_index[None, None, :] <= row_index[None, :, None]) & (
        key_index[None, None, :] >= row_first[:, :, None]
    )
    scores = dot("vqgrd,vkgd->vgrqk", grouped, keys) * HD**-0.5
    scores = jnp.where(allowed[:, None, None], scores, -1e30)
    probs = jnp.exp(scores - jnp.max(scores, axis=-1, keepdims=True))
    probs = probs / jnp.sum(probs, axis=-1, keepdims=True)
    attended = dot("vgrqk,vkgd->vqgrd", probs.astype(bf16), values).astype(bf16)
    attended = own_halves(core, attended.reshape(sequences, count, heads * HD))
    out, sent = project_out(team, "tc,dc->td", attended, weights[:, inner:])
    stored = (
        inverse,
        normed,
        tokens,
        query_inverse,
        query_normed,
        key_inverse,
        key_normed,
        cosines,
        sines,
        grouped,
        keys,
        values,
        probs,
        attended,
    )
    return hidden + out, stored, mixed


def attend_backward(team, core, back_out, stored, gain, weights, query_gain, key_gain, before):
    (
        inverse,
        normed,
        tokens,
        query_inverse,
        query_normed,
        key_inverse,
        key_normed,
        cosines,
        sines,
        grouped,
        keys,
        values,
        probs,
        attended,
    ) = stored
    sequences, count, groups, repeat = grouped.shape[:4]
    heads = groups * repeat
    inner = (heads + 2 * groups) * HD
    back_tokens = gather_tokens(team, back_out.astype(bf16))
    back_attended = true_order(core, team.size, project("td,dc->tc", back_tokens, held(weights[:, inner:], before[0]))).astype(bf16)
    back_grouped = back_attended.reshape(sequences, count, groups, repeat, HD)
    back_probs = dot("vqgrd,vkgd->vgrqk", back_grouped, values)
    row_dot = jnp.sum(probs * back_probs, axis=-1, keepdims=True)
    back_scores = (probs * (back_probs - row_dot)).astype(bf16)
    back_query_rot = dot("vgrqk,vkgd->vqgrd", back_scores, keys) * HD**-0.5
    back_keys = dot("vgrqk,vqgrd->vkgd", back_scores, grouped) * HD**-0.5
    back_values = dot("vgrqk,vqgrd->vkgd", probs.astype(bf16), back_grouped)
    back_slots = jnp.concatenate(
        [
            back_keys.reshape(sequences, -1, count, groups * HD),
            back_values.reshape(sequences, -1, count, groups * HD),
        ],
        axis=-1,
    )
    back_pair = back_slots[:, 0]
    for i in range(1, back_slots.shape[1]):
        back_pair = back_pair + shift(back_slots[:, i].astype(bf16), -i).astype(f32)
    back_query_scaled = rotate(back_query_rot.reshape(sequences, count, heads, HD), cosines, -sines)
    query_scale_term = jnp.sum(back_query_scaled * query_normed, axis=(0, 1, 2))
    back_query = norm_back(back_query_scaled * query_gain, query_normed, query_inverse)
    back_key_rot = back_pair[..., : groups * HD].reshape(sequences, count, groups, HD)
    back_key_scaled = rotate(back_key_rot, cosines, -sines)
    key_scale_term = jnp.sum(back_key_scaled * key_normed, axis=(0, 1, 2))
    back_key = norm_back(back_key_scaled * key_gain, key_normed, key_inverse)
    back_mixed = jnp.concatenate(
        [
            back_query.reshape(sequences, count, heads * HD),
            back_key.reshape(sequences, count, groups * HD),
            back_pair[..., groups * HD :],
        ],
        axis=-1,
    ).astype(bf16)
    back_mixed = own_halves(core, back_mixed)
    back_normed, sent = project_out(team, "tc,dc->td", back_mixed, held(weights[:, :inner], before[1]))
    term = jnp.concatenate([outer(tokens, back_mixed), outer(back_tokens, attended)], axis=-1)
    back_hidden, gain_term = after_norm(back_out, back_normed, normed, inverse, gain)
    return back_hidden, gain_term, term, (query_scale_term, key_scale_term), back_attended


def grid_total(array):
    for axis in ("dp", "seq"):
        mask = 1
        while mask < lax.axis_size(axis):
            array = array + swap(array, axis, mask)
            mask *= 2
    return array


def body(
    hidden_in,
    positions,
    mixer_gain,
    mixer_in,
    mixer_taps,
    mixer_out,
    first_gain,
    first_lift,
    first_drop,
    attend_gain,
    query_weight,
    pair_weight,
    query_scale,
    key_scale,
    attend_out,
    second_gain,
    second_lift,
    second_drop,
    cotangent,
):
    core = lax.axis_index("mp")
    team = Team("dp")
    first_team, second_team = Team(FIRST_AXIS), Team(SECOND_AXIS)
    rank = lax.axis_index("dp") * lax.axis_size("seq") + lax.axis_index("seq")
    model = hidden_in.shape[-1]
    share = hidden_in.shape[1] // 2
    own_tokens = lax.dynamic_slice_in_dim(hidden_in[0], core * share, share)
    hidden = own_tokens.astype(f32)
    signal_low = lax.dynamic_slice_in_dim(cotangent[0], core * share, share)
    signal = signal_low.astype(f32)
    query_gain, key_gain = query_scale.astype(f32), key_scale.astype(f32)
    channels = mixer_taps.shape[1] // team.size
    taps = lax.dynamic_slice_in_dim(mixer_taps, team.seat * channels, channels, 1).astype(f32)
    units = first_drop.shape[1]
    first_mask = hidden_mask(units, first_team.size, first_team.seat)
    second_mask = hidden_mask(units, second_team.size, second_team.seat)

    def feed_piece(on, lift, drop, late):
        width = hidden_width(units, on.size)

        def piece(seat):
            start = hidden_start(units, on.size, seat) + late
            parts = [lift[:, 0], lift[:, 1], drop]
            return jnp.concatenate([lax.dynamic_slice_in_dim(part, start, width, 1) for part in parts], axis=1)

        return piece

    def lift_of(pieces):
        return [piece[:, : 2 * piece.shape[1] // 3] for piece in pieces]

    def drop_of(pieces):
        return [piece[:, 2 * piece.shape[1] // 3 :] for piece in pieces]

    token_halves = gather_tokens(team, own_tokens)
    packed = pack_mixer(mixer_in, mixer_out)
    got = team_rows(team, lambda seat: take(packed, seat, 0))
    mixer_weights = all_rows(team, got)
    near_done = zero(got[-1])

    got_first = team_rows(first_team, feed_piece(first_team, first_lift, first_drop, near_done))
    first_lift_all = all_rows(first_team, lift_of(got_first))
    first_drop_all = all_rows(first_team, drop_of(got_first))
    near_done = zero(got_first[-1])

    gain_rows = mixer_gain.shape[0]
    gains = jnp.stack([mixer_gain, first_gain, attend_gain, second_gain]).astype(f32)
    gains = grid_total(
        lax.dynamic_update_slice_in_dim(jnp.zeros((4, model), f32), gains, rank * gain_rows + near_done, 1)
    )
    own_places = positions[0] + near_done
    order = jnp.stack([own_places] + [swap(own_places, team.axis, mask) for mask in range(1, team.size)])

    packed_attend = pack_attend(query_weight, pair_weight, attend_out)
    got_attend = team_rows(team, lambda seat: take(packed_attend, seat + near_done, 0))
    got_second = team_rows(second_team, feed_piece(second_team, second_lift, second_drop, near_done))

    after_mixer, mixer_stored, parts = mixer_forward(
        team, core, hidden, token_halves, order, gains[0], mixer_weights, taps
    )
    mixed_done = zero(parts)
    attend_weights = all_rows(team, got_attend, mixed_done)
    second_lift_all = all_rows(second_team, lift_of(got_second), mixed_done)
    second_drop_all = all_rows(second_team, drop_of(got_second), mixed_done)

    first_stored = feed_forward(first_team, after_mixer, gains[1], first_lift_all, first_mask)
    out, sent = project_out(first_team, "tf,df->td", first_stored[-1], first_drop_all)
    after_first = after_mixer + out
    after_attend, attend_stored, mixed = attend_forward(
        team, core, after_first, order, gains[2], attend_weights, query_gain, key_gain
    )
    signal_low = signal_low + zero(mixed).astype(bf16)
    signal_tokens = gather_tokens(second_team, signal_low)
    second_stored = feed_forward(second_team, after_attend, gains[3], second_lift_all, second_mask)

    back, second_gain_term, *second_part = feed_backward(
        second_team, signal, signal_tokens, second_stored, gains[3], second_lift_all, second_drop_all, second_mask, False
    )
    back, attend_gain_term, attend_term, scale_terms, back_attended = attend_backward(
        team, core, back, attend_stored, gains[2], attend_weights, query_gain, key_gain, second_part
    )
    attend_part = summed_rows(team, attend_term)
    late = zero(back_attended).astype(bf16)
    out, sent = project_out(second_team, "tf,df->td", [half + late for half in second_stored[-1]], second_drop_all)
    result = after_attend + out

    first_back_tokens = gather_tokens(first_team, back.astype(bf16))
    back, first_gain_term, *first_part = feed_backward(
        first_team, back, first_back_tokens, first_stored, gains[1], first_lift_all, first_drop_all, held(first_mask, attend_part), True
    )
    back, mixer_gain_term, mixer_term, tap_term, back_gated = mixer_backward(
        team, core, back, mixer_stored, gains[0], mixer_weights, taps
    )
    mixer_part = summed_rows(team, mixer_term)
    gated_done = zero(back_gated)
    second_total = every_seat(second_team, jnp.concatenate(second_part[::-1], axis=-1), gated_done)
    attend_total = every_seat(team, attend_part, gated_done)
    first_total = every_seat(first_team, jnp.concatenate(first_part[::-1], axis=-1))
    mixer_total = every_seat(team, mixer_part)

    small = jnp.concatenate(
        [mixer_gain_term, first_gain_term, attend_gain_term, second_gain_term, scale_terms[0], scale_terms[1]]
    )
    small = small + swap_core(small)
    tap_full = lax.dynamic_update_slice_in_dim(
        jnp.zeros((3, mixer_taps.shape[1]), f32), tap_term, team.seat * channels, 1
    )
    small = grid_total(jnp.concatenate([small, tap_full.reshape(-1)]))
    gain_totals = lax.dynamic_slice_in_dim(
        small[: 4 * model].reshape(4, model), rank * gain_rows, gain_rows, 1
    )
    scale_totals = small[4 * model : 4 * model + 2 * HD].reshape(2, HD)
    tap_total = small[4 * model + 2 * HD :].reshape(tap_full.shape)

    def both_cores(own):
        return true_order(core, 1, [own, swap_core(own)])

    def joined_lift(total):
        width = total.shape[-1] // 3
        return jnp.stack([joined_hidden(units, total[..., k * width : (k + 1) * width]) for k in range(2)], axis=1)

    def joined_drop(total):
        return joined_hidden(units, total[..., 2 * total.shape[-1] // 3 :])

    rows = mixer_in.shape[0]
    in_columns = 3 * channels
    inner = attend_total.shape[-1] - query_weight.shape[1] // 4
    queries = query_weight.shape[1] // 4
    return (
        both_cores(result.astype(bf16)),
        both_cores(back),
        gain_totals[0],
        all_seats(mixer_total[..., :in_columns].reshape(4, rows, 3, channels)),
        tap_total,
        all_seats(mixer_total[..., in_columns:]),
        gain_totals[1],
        joined_lift(first_total),
        joined_drop(first_total),
        gain_totals[2],
        all_seats(attend_total[..., :queries]),
        all_seats(attend_total[..., queries:inner].reshape(4, rows, 2, -1)),
        scale_totals[0],
        scale_totals[1],
        all_seats(attend_total[..., inner:]),
        gain_totals[3],
        joined_lift(second_total),
        joined_drop(second_total),
    )


def solution(mesh):
    grid = ("dp", "seq")
    return jax.shard_map(
        body,
        mesh=mesh,
        in_specs=(
            P("dp", "seq", None),
            P("dp", "seq"),
            P(grid),
            P(grid, None, "mp"),
            P(None, "mp"),
            P(grid, "mp"),
            P(grid),
            P(grid, None, "mp"),
            P(grid, "mp"),
            P(grid),
            P(grid, "mp"),
            P(grid, None, "mp"),
            P(),
            P(),
            P(grid, "mp"),
            P(grid),
            P(grid, None, "mp"),
            P(grid, "mp"),
            P("dp", "seq", None),
        ),
        out_specs=(
            P("dp", "seq", None),
            P("dp", "seq", None),
            P(grid),
            P(grid, None, "mp"),
            P(None, "mp"),
            P(grid, "mp"),
            P(grid),
            P(grid, None, "mp"),
            P(grid, "mp"),
            P(grid),
            P(grid, "mp"),
            P(grid, None, "mp"),
            P(),
            P(),
            P(grid, "mp"),
            P(grid),
            P(grid, None, "mp"),
            P(grid, "mp"),
        ),
        check_vma=False,
    )
```

```python
import jax
import jax.numpy as jnp
from jax import lax
from jax.experimental import pallas as pl
from jax.experimental.pallas import tpu as pltpu
from jax.sharding import PartitionSpec as P

HD = 64

epsilon = 1e-05
rope_base = 1000000.0
bf16 = jnp.bfloat16
f32 = jnp.float32


def rms_scale(values):
    return lax.rsqrt(jnp.mean(values * values, axis=-1, keepdims=True) + epsilon)


def norm_back(back_normed, normed, inverse):
    return inverse * (back_normed - normed * jnp.mean(back_normed * normed, axis=-1, keepdims=True))


def frequencies():
    exponent = jnp.arange(HD // 2, dtype=f32) * (2.0 / HD)
    return jnp.power(rope_base, -exponent)


def rotate(values, cosines, sine_table):
    middle = values.shape[-1] // 2
    leading = values[..., :middle]
    trailing = values[..., middle:]
    return jnp.concatenate(
        [leading * cosines - trailing * sine_table, trailing * cosines + leading * sine_table],
        axis=-1,
    )


def dot(pattern, first, second):
    return jnp.einsum(pattern, first, second, preferred_element_type=f32)


class Team:
    def __init__(self, axis):
        self.axis = axis
        self.across = "seq" if axis == "dp" else "dp"
        self.size = lax.axis_size(axis)
        self.seat = lax.axis_index(axis)


def swap(array, axis, mask):
    return lax.ppermute(array, axis, [(i, i ^ mask) for i in range(lax.axis_size(axis))])


def swap_core(array):
    return swap(array, "mp", 1)


def shift(array, by):
    count = lax.axis_size("seq")
    return lax.ppermute(array, "seq", [(i, i + by) for i in range(count) if 0 <= i + by < count])


def zero(token):
    element = token[(0,) * token.ndim].astype(f32)
    return (element * 0.0).astype(jnp.int32)


def take(array, index, axis):
    return lax.dynamic_index_in_dim(array, index, axis, keepdims=False)


def gather_tokens(team, own):
    mine = jnp.concatenate([own] + [swap(own, team.axis, mask) for mask in range(1, team.size)], axis=0)
    return mine, swap_core(mine)


def scatter_begin(team, mine, other):
    received = swap_core(other.astype(bf16)).astype(f32)
    rows = mine.shape[0] // team.size
    both = mine + received
    sends = [(mask, both[mask * rows : (mask + 1) * rows].astype(bf16)) for mask in range(team.size - 1, 0, -1)]
    return both[:rows], sends


def scatter_end(team, total, sends):
    received = [swap(send, team.axis, mask) for mask, send in sends]
    for array in received:
        total = total + array.astype(f32)
    return total


def scatter_tokens(team, mine, other):
    total, sends = scatter_begin(team, mine, other)
    return scatter_end(team, total, sends), sends[-1][1]


def true_order(core, sequences, halves):
    mine, other = (half.reshape(sequences, -1, half.shape[-1]) for half in halves)
    return jnp.where(
        core == 0, jnp.concatenate([mine, other], axis=1), jnp.concatenate([other, mine], axis=1)
    )


def own_halves(core, ordered):
    rows = ordered.shape[1] // 2
    return [
        lax.dynamic_slice_in_dim(ordered, at * rows, rows, 1).reshape(-1, ordered.shape[-1])
        for at in (core, 1 - core)
    ]


def team_rows(team, piece_of):
    return [
        swap(piece_of(team.seat ^ mask), team.axis, mask) if mask else piece_of(team.seat)
        for mask in range(team.size)
    ]


def all_rows(team, pieces, late=0):
    lead, (rows, columns) = pieces[0].shape[:-2], pieces[0].shape[-2:]
    plain = (0,) * len(lead)
    near = jnp.zeros(lead + (team.size, rows, columns), pieces[0].dtype)
    for mask, piece in enumerate(pieces):
        near = lax.dynamic_update_slice(
            near, jnp.expand_dims(piece, len(lead)), plain + ((team.seat ^ mask) + late, 0, 0)
        )
    if team.axis == "dp":
        whole = lax.all_gather(near, team.across, axis=len(lead) + 1, tiled=True)
    else:
        near = near.reshape(lead + (team.size * rows, columns))
        whole = lax.all_gather(near, team.across, axis=len(lead), tiled=True)
    return whole.reshape(lead + (-1, columns))


def summed_rows(team, gradient):
    columns = gradient.shape[-1]
    teams = lax.axis_size(team.across)
    if team.axis == "dp":
        split = gradient.reshape(team.size, teams, -1, columns).swapaxes(0, 1)
    else:
        split = gradient.reshape(teams, team.size, -1, columns)
    rows = split.shape[2]
    part = lax.psum_scatter(split.reshape(-1, columns), team.across, scatter_dimension=0, tiled=True)
    return part.reshape(team.size, rows, columns)


def every_seat(team, part, late=0):
    axis = part.ndim - 3
    pieces = []
    for mask in range(team.size):
        piece = take(part, (team.seat ^ mask) + late, axis)
        pieces.append(swap(piece, team.axis, mask) if mask else piece)
    seats = jnp.stack(pieces)
    shape, bits = seats.shape, team.size.bit_length() - 1
    seats = seats.reshape((2,) * bits + shape[1:])
    for bit in range(bits):
        seats = jnp.where((team.seat >> bit) & 1 == 1, jnp.flip(seats, bits - 1 - bit), seats)
    return seats.reshape(shape).astype(f32)


def hidden_width(units, seats):
    tiles = -(-units // (128 * seats))
    return tiles * 128 if units % 128 == 0 else units // seats


def hidden_start(units, seats, seat):
    width = hidden_width(units, seats)
    return jnp.minimum(seat * width, units - width)


def hidden_mask(units, seats, seat):
    width = hidden_width(units, seats)
    doubled = seat * width - hidden_start(units, seats, seat)
    return (lax.broadcasted_iota(jnp.int32, (1, width), 1) >= doubled).astype(f32)


def joined_hidden(units, pieces):
    seats = len(pieces)
    width = hidden_width(units, seats)
    parts = []
    for seat in range(seats):
        low, start = seat * width, min(seat * width, units - width)
        if low < units:
            parts.append(pieces[seat][..., low - start : min(low + width, units) - start])
    return jnp.concatenate(parts, axis=-1)


def quarter(array, seat):
    width = array.shape[-1] // 4
    return array[..., seat * width : (seat + 1) * width]


def all_seats(array):
    return jnp.concatenate([array[i] for i in range(4)], axis=-1)


def pack_mixer(weight_in, weight_out):
    seats = [
        jnp.concatenate([quarter(weight_in[:, k], i) for k in range(3)] + [quarter(weight_out, i)], axis=-1)
        for i in range(4)
    ]
    return jnp.stack(seats)


def pack_attend(query_weight, pair_weight, out_weight):
    seats = [
        jnp.concatenate(
            [quarter(query_weight, i)]
            + [quarter(pair_weight[:, k], i) for k in range(2)]
            + [quarter(out_weight, i)],
            axis=-1,
        )
        for i in range(4)
    ]
    return jnp.stack(seats)


def lowered_norm(hidden, gain):
    inverse = rms_scale(hidden)
    normed = hidden * inverse
    return inverse, normed, (normed * gain).astype(bf16)


def after_norm(back_out, back_normed, normed, inverse, gain):
    gain_term = jnp.sum(back_normed * normed, axis=0)
    return back_out + norm_back(back_normed * gain, normed, inverse), gain_term


def project(pattern, halves, weights):
    return [dot(pattern, half, weights) for half in halves]


def project_out(team, pattern, halves, weights):
    other = dot(pattern, halves[1], weights)
    mine = dot(pattern, halves[0], weights)
    return scatter_tokens(team, mine, other)


def outer(first, second):
    return (dot("td,tf->df", first[0], second[0]) + dot("td,tf->df", first[1], second[1])).astype(bf16)


def feed_active(tokens, lift, mask):
    both = dot("td,df->tf", tokens, lift)
    width = both.shape[1] // 2
    gate, up = both[:, :width], both[:, width:]
    return gate, up, (jax.nn.silu(gate) * up * mask).astype(bf16)


def feed_back(back_tokens, gate, up, drop, mask):
    back_active = dot("td,df->tf", back_tokens, drop) * mask
    sigmoid_value = jax.nn.sigmoid(gate)
    back_gate = back_active * up * sigmoid_value * (1.0 + gate * (1.0 - sigmoid_value))
    return jnp.concatenate([back_gate, back_active * gate * sigmoid_value], axis=1).astype(bf16)


def feed_forward(team, hidden, gain, lift, mask):
    inverse, normed, lowered = lowered_norm(hidden, gain)
    tokens = gather_tokens(team, lowered)
    gate, up, active = zip(*[feed_active(half, lift, mask) for half in tokens])
    return inverse, normed, tokens, gate, up, active


def held(array, token):
    return array + zero(token).astype(array.dtype)


def feed_backward(team, back_out, back_tokens, stored, gain, lift, drop, mask, hold):
    inverse, normed, tokens, gate, up, active = stored
    back_pair = [feed_back(back_tokens[i], gate[i], up[i], drop, mask) for i in range(2)]
    back_normed, sent = project_out(team, "tf,df->td", back_pair, lift)
    drop_part = summed_rows(team, outer(back_tokens, active))
    lift_part = summed_rows(team, outer(tokens, back_pair))
    if hold is not None:
        gain = held(held(gain, drop_part), hold)
    back_hidden, gain_term = after_norm(back_out, back_normed, normed, inverse, gain)
    return back_hidden, gain_term, drop_part, lift_part


def mixer_forward(team, core, hidden, token_halves, order, gain, weights, taps):
    inverse = rms_scale(hidden)
    normed = hidden * inverse
    tokens = [lowered_norm(half.astype(f32), gain)[2] for half in token_halves]
    channels = taps.shape[1]
    parts = true_order(core, team.size, project("td,dc->tc", tokens, weights[:, : 3 * channels]))
    gate_in, gate_out, value = (parts[..., i * channels : (i + 1) * channels] for i in range(3))
    mixed = (gate_in * value).astype(bf16)
    earlier = shift(mixed[:, -2:], 1)
    padded = jnp.concatenate([earlier, mixed], axis=1).astype(f32)
    one_back = (order >= 1).astype(f32)[..., None]
    two_back = (order >= 2).astype(f32)[..., None]
    convolved = (
        taps[2] * padded[:, 2:] + taps[1] * padded[:, 1:-1] * one_back + taps[0] * padded[:, :-2] * two_back
    )
    gated = own_halves(core, (gate_out * convolved).astype(bf16))
    out, sent = project_out(team, "tc,dc->td", gated, weights[:, 3 * channels :])
    stored = (inverse, normed, tokens, gate_in, gate_out, value, padded, convolved, gated, one_back, two_back)
    return hidden + out, stored, parts


def mixer_backward(team, core, back_out, stored, gain, weights, taps):
    inverse, normed, tokens, gate_in, gate_out, value, padded, convolved, gated, one_back, two_back = stored
    channels = taps.shape[1]
    back_tokens = gather_tokens(team, back_out.astype(bf16))
    back_gated = true_order(core, team.size, project("td,dc->tc", back_tokens, weights[:, 3 * channels :]))
    back_conv = back_gated * gate_out
    back_padded = (
        jnp.pad(taps[2] * back_conv, ((0, 0), (2, 0), (0, 0)))
        + jnp.pad(taps[1] * back_conv * one_back, ((0, 0), (1, 1), (0, 0)))
        + jnp.pad(taps[0] * back_conv * two_back, ((0, 0), (0, 2), (0, 0)))
    )
    later = shift(back_padded[:, :2], -1)
    back_mixed = back_padded[:, 2:] + jnp.pad(later, ((0, 0), (back_conv.shape[1] - 2, 0), (0, 0)))
    back_parts = own_halves(
        core,
        jnp.concatenate(
            [back_mixed * value, back_gated * convolved, back_mixed * gate_in], axis=-1
        ).astype(bf16),
    )
    back_normed, sent = project_out(team, "tc,dc->td", back_parts, weights[:, : 3 * channels])
    tap_term = jnp.stack(
        [
            jnp.sum(back_conv * padded[:, :-2] * two_back, axis=(0, 1)),
            jnp.sum(back_conv * padded[:, 1:-1] * one_back, axis=(0, 1)),
            jnp.sum(back_conv * padded[:, 2:], axis=(0, 1)),
        ]
    )
    term = jnp.concatenate([outer(tokens, back_parts), outer(back_tokens, gated)], axis=-1)
    back_hidden, gain_term = after_norm(back_out, back_normed, normed, inverse, gain)
    return back_hidden, gain_term, term, tap_term, back_gated


def turned(first, second):
    return lax.dot_general(first, second, (((1,), (1,)), ((), ())), preferred_element_type=f32)


def summed(first, second):
    return lax.dot_general(first, second, (((0,), (0,)), ((), ())), preferred_element_type=f32)


def allowed_keys(base_ref, order_ref, keys, count):
    base = base_ref[0]
    slot_row = lax.broadcasted_iota(jnp.int32, (keys, 1), 0)
    slot = lax.div(slot_row, count)
    key_index = base + slot_row - 2 * slot * count
    query_index = base + lax.broadcasted_iota(jnp.int32, (1, count), 1)
    return (key_index <= query_index) & (key_index >= query_index - order_ref[0])


def key_probs(query, keys, allowed):
    scores = jnp.where(allowed, turned(keys, query) * HD**-0.5, -1e30)
    weights = jnp.exp(scores - jnp.max(scores, axis=0, keepdims=True))
    return weights * (1.0 / jnp.sum(weights, axis=0, keepdims=True))


def attend_kernel(base_ref, order_ref, query_ref, slots_ref, out_ref):
    count, keys = query_ref.shape[1], slots_ref.shape[1]
    allowed = allowed_keys(base_ref, order_ref, keys, count)
    key, value = slots_ref[0, :, :HD], slots_ref[0, :, HD:]
    parts = []
    for head in range(query_ref.shape[2] // HD):
        query = query_ref[0, :, head * HD : (head + 1) * HD]
        probs = key_probs(query, key, allowed)
        parts.append(summed(probs.astype(bf16), value))
    out_ref[0] = jnp.concatenate(parts, axis=1).astype(bf16)


def attend_back_kernel(base_ref, order_ref, query_ref, back_ref, slots_ref, back_query_ref, own_ref, rest_ref):
    count, keys = query_ref.shape[1], slots_ref.shape[1]
    allowed = allowed_keys(base_ref, order_ref, keys, count)
    key, value = slots_ref[0, :, :HD], slots_ref[0, :, HD:]
    back_queries = []
    back_key = jnp.zeros((keys, HD), f32)
    back_value = jnp.zeros((keys, HD), f32)
    for head in range(query_ref.shape[2] // HD):
        query = query_ref[0, :, head * HD : (head + 1) * HD]
        back = back_ref[0, :, head * HD : (head + 1) * HD]
        probs = key_probs(query, key, allowed)
        back_probs = turned(value, back)
        row_dot = jnp.sum(probs * back_probs, axis=0, keepdims=True)
        back_scores = (probs * (back_probs - row_dot)).astype(bf16)
        back_queries.append(summed(back_scores, key) * HD**-0.5)
        back_key += jnp.dot(back_scores, query, preferred_element_type=f32)
        back_value += jnp.dot(probs.astype(bf16), back, preferred_element_type=f32)
    back_query_ref[0] = jnp.concatenate(back_queries, axis=1)
    back_pair = jnp.concatenate([back_key * HD**-0.5, back_value], axis=1)
    own_ref[0] = back_pair[:count]
    rest_ref[0] = back_pair[count:].astype(bf16)


def attend_call(kernel, base, order, arrays, outs):
    sequences, count = order.shape

    def block(shape):
        return pl.BlockSpec((1,) + tuple(shape[1:]), lambda i: (i, 0, 0))

    keys = arrays[-1].shape[1]
    heads = arrays[0].shape[2] // HD
    return pl.pallas_call(
        kernel,
        grid=(sequences,),
        in_specs=[pl.BlockSpec(memory_space=pltpu.SMEM), block((sequences, 1, count))]
        + [block(array.shape) for array in arrays],
        out_specs=[block(out.shape) for out in outs],
        out_shape=outs,
        compiler_params=pltpu.CompilerParams(vmem_limit_bytes=56 * 1024 * 1024),
        cost_estimate=pl.CostEstimate(
            flops=10 * sequences * heads * count * keys * HD,
            bytes_accessed=sum(2 * array.size for array in arrays),
            transcendentals=sequences * heads * count * keys,
        ),
    )(base.reshape(1), order.reshape(sequences, 1, count), *arrays)


def attend_forward(team, core, hidden, order, gain, weights, query_gain, key_gain):
    inverse, normed, lowered = lowered_norm(hidden, gain)
    tokens = gather_tokens(team, lowered)
    heads = weights.shape[1] * 3 // 8 // HD
    groups = weights.shape[1] // 8 // HD
    repeat = heads // groups
    inner = (heads + 2 * groups) * HD
    mixed = true_order(core, team.size, project("td,dc->tc", tokens, weights[:, :inner]))
    sequences, count = mixed.shape[:2]
    query_heads = mixed[..., : heads * HD].reshape(sequences, count, heads, HD)
    key_heads = mixed[..., heads * HD : (heads + groups) * HD].reshape(sequences, count, groups, HD)
    value_low = mixed[..., (heads + groups) * HD :].astype(bf16)
    angles = order.astype(f32)[..., None] * frequencies()
    cosines, sines = jnp.cos(angles)[:, :, None, :], jnp.sin(angles)[:, :, None, :]
    query_inverse = rms_scale(query_heads)
    query_normed = query_heads * query_inverse
    query_rot = rotate(query_normed * query_gain, cosines, sines).astype(bf16)
    key_inverse = rms_scale(key_heads)
    key_normed = key_heads * key_inverse
    key_rot = rotate(key_normed * key_gain, cosines, sines).astype(bf16)
    pair = jnp.concatenate([key_rot.reshape(sequences, count, groups * HD), value_low], axis=-1)
    blocks = lax.axis_size("seq")
    here = lax.axis_index("seq")
    slots = jnp.concatenate([shift(pair, i) if i else pair for i in range(blocks)], axis=1)
    base = (here * count).astype(jnp.int32)
    query_rot = query_rot.reshape(sequences, count, heads * HD)
    (attended,) = attend_call(
        attend_kernel, base, order, [query_rot, slots], [jax.ShapeDtypeStruct((sequences, count, heads * HD), bf16)]
    )
    attended = own_halves(core, attended)
    out, sent = project_out(team, "tc,dc->td", attended, weights[:, inner:])
    stored = (
        inverse,
        normed,
        tokens,
        query_inverse,
        query_normed,
        key_inverse,
        key_normed,
        cosines,
        sines,
        query_rot,
        slots,
        base,
        order,
        attended,
    )
    return hidden + out, stored, mixed


def attend_backward(team, core, back_out, stored, gain, weights, query_gain, key_gain, before):
    (
        inverse,
        normed,
        tokens,
        query_inverse,
        query_normed,
        key_inverse,
        key_normed,
        cosines,
        sines,
        query_rot,
        slots,
        base,
        order,
        attended,
    ) = stored
    sequences, count = query_rot.shape[:2]
    heads, groups = query_rot.shape[2] // HD, slots.shape[2] // (2 * HD)
    inner = (heads + 2 * groups) * HD
    back_tokens = gather_tokens(team, back_out.astype(bf16))
    back_attended = true_order(core, team.size, project("td,dc->tc", back_tokens, held(weights[:, inner:], before[0]))).astype(bf16)
    back_query_rot, back_pair, rest = attend_call(
        attend_back_kernel,
        base,
        order,
        [query_rot, back_attended, slots],
        [
            jax.ShapeDtypeStruct((sequences, count, heads * HD), f32),
            jax.ShapeDtypeStruct((sequences, count, 2 * HD), f32),
            jax.ShapeDtypeStruct((sequences, slots.shape[1] - count, 2 * HD), bf16),
        ],
    )
    for i in range(1, slots.shape[1] // count):
        back_pair = back_pair + shift(rest[:, (i - 1) * count : i * count], -i).astype(f32)
    back_query_scaled = rotate(back_query_rot.reshape(sequences, count, heads, HD), cosines, -sines)
    query_scale_term = jnp.sum(back_query_scaled * query_normed, axis=(0, 1, 2))
    back_query = norm_back(back_query_scaled * query_gain, query_normed, query_inverse)
    back_key_rot = back_pair[..., : groups * HD].reshape(sequences, count, groups, HD)
    back_key_scaled = rotate(back_key_rot, cosines, -sines)
    key_scale_term = jnp.sum(back_key_scaled * key_normed, axis=(0, 1, 2))
    back_key = norm_back(back_key_scaled * key_gain, key_normed, key_inverse)
    back_mixed = jnp.concatenate(
        [
            back_query.reshape(sequences, count, heads * HD),
            back_key.reshape(sequences, count, groups * HD),
            back_pair[..., groups * HD :],
        ],
        axis=-1,
    ).astype(bf16)
    back_mixed = own_halves(core, back_mixed)
    back_normed, sent = project_out(team, "tc,dc->td", back_mixed, held(weights[:, :inner], before[1]))
    term = jnp.concatenate([outer(tokens, back_mixed), outer(back_tokens, attended)], axis=-1)
    back_hidden, gain_term = after_norm(back_out, back_normed, normed, inverse, gain)
    return back_hidden, gain_term, term, (query_scale_term, key_scale_term), back_attended


def grid_total(array):
    for axis in ("dp", "seq"):
        mask = 1
        while mask < lax.axis_size(axis):
            array = array + swap(array, axis, mask)
            mask *= 2
    return array


def body(
    hidden_in,
    positions,
    mixer_gain,
    mixer_in,
    mixer_taps,
    mixer_out,
    first_gain,
    first_lift,
    first_drop,
    attend_gain,
    query_weight,
    pair_weight,
    query_scale,
    key_scale,
    attend_out,
    second_gain,
    second_lift,
    second_drop,
    cotangent,
):
    core = lax.axis_index("mp")
    team = Team("dp")
    first_team = second_team = team
    rank = lax.axis_index("dp") * lax.axis_size("seq") + lax.axis_index("seq")
    model = hidden_in.shape[-1]
    share = hidden_in.shape[1] // 2
    own_tokens = lax.dynamic_slice_in_dim(hidden_in[0], core * share, share)
    hidden = own_tokens.astype(f32)
    signal_low = lax.dynamic_slice_in_dim(cotangent[0], core * share, share)
    signal = signal_low.astype(f32)
    query_gain, key_gain = query_scale.astype(f32), key_scale.astype(f32)
    channels = mixer_taps.shape[1] // team.size
    taps = lax.dynamic_slice_in_dim(mixer_taps, team.seat * channels, channels, 1).astype(f32)
    units = first_drop.shape[1]
    first_mask = hidden_mask(units, first_team.size, first_team.seat)
    second_mask = hidden_mask(units, second_team.size, second_team.seat)

    def feed_piece(on, lift, drop, late):
        width = hidden_width(units, on.size)

        def piece(seat):
            start = hidden_start(units, on.size, seat) + late
            parts = [lift[:, 0], lift[:, 1], drop]
            return jnp.concatenate([lax.dynamic_slice_in_dim(part, start, width, 1) for part in parts], axis=1)

        return piece

    def lift_of(pieces):
        return [piece[:, : 2 * piece.shape[1] // 3] for piece in pieces]

    def drop_of(pieces):
        return [piece[:, 2 * piece.shape[1] // 3 :] for piece in pieces]

    token_halves = gather_tokens(team, own_tokens)
    packed = pack_mixer(mixer_in, mixer_out)
    got = team_rows(team, lambda seat: take(packed, seat, 0))
    mixer_weights = all_rows(team, got)
    near_done = zero(got[-1])

    got_first = team_rows(first_team, feed_piece(first_team, first_lift, first_drop, near_done))
    first_lift_all = all_rows(first_team, lift_of(got_first))
    first_drop_all = all_rows(first_team, drop_of(got_first))
    near_done = zero(got_first[-1])

    gain_rows = mixer_gain.shape[0]
    gains = jnp.stack([mixer_gain, first_gain, attend_gain, second_gain]).astype(f32)
    gains = grid_total(
        lax.dynamic_update_slice_in_dim(jnp.zeros((4, model), f32), gains, rank * gain_rows + near_done, 1)
    )
    own_places = positions[0] + near_done
    order = jnp.stack([own_places] + [swap(own_places, team.axis, mask) for mask in range(1, team.size)])

    packed_attend = pack_attend(query_weight, pair_weight, attend_out)
    got_attend = team_rows(team, lambda seat: take(packed_attend, seat + near_done, 0))
    got_second = team_rows(second_team, feed_piece(second_team, second_lift, second_drop, near_done))

    after_mixer, mixer_stored, parts = mixer_forward(
        team, core, hidden, token_halves, order, gains[0], mixer_weights, taps
    )
    mixed_done = zero(parts)
    beside = [jnp.concatenate(pair, axis=1) for pair in zip(got_attend, drop_of(got_second))]
    shared = all_rows(team, beside, mixed_done)
    attend_weights, second_drop_all = shared[:, : got_attend[0].shape[1]], shared[:, got_attend[0].shape[1] :]
    second_lift_all = all_rows(second_team, lift_of(got_second), mixed_done)

    first_stored = feed_forward(first_team, after_mixer, gains[1], first_lift_all, first_mask)
    out, sent = project_out(first_team, "tf,df->td", first_stored[-1], first_drop_all)
    after_first = after_mixer + out
    after_attend, attend_stored, mixed = attend_forward(
        team, core, after_first, order, gains[2], attend_weights, query_gain, key_gain
    )
    signal_low = signal_low + zero(mixed).astype(bf16)
    signal_tokens = gather_tokens(second_team, signal_low)
    second_stored = feed_forward(second_team, after_attend, gains[3], second_lift_all, second_mask)

    result_sums, result_sends = scatter_begin(
        second_team, *project("tf,df->td", second_stored[-1], second_drop_all)
    )
    second_mask = held(second_mask, result_sends[-1][1])

    back, second_gain_term, *second_part = feed_backward(
        second_team, signal, signal_tokens, second_stored, gains[3], second_lift_all, second_drop_all, second_mask, None
    )
    back, attend_gain_term, attend_term, scale_terms, back_attended = attend_backward(
        team, core, back, attend_stored, gains[2], attend_weights, query_gain, key_gain, second_part
    )
    attend_part = summed_rows(team, attend_term)
    result = after_attend + scatter_end(second_team, held(result_sums, back_attended), result_sends)

    first_back_tokens = gather_tokens(first_team, back.astype(bf16))
    back, first_gain_term, *first_part = feed_backward(
        first_team, back, first_back_tokens, first_stored, gains[1], first_lift_all, first_drop_all, first_mask, attend_part
    )
    back, mixer_gain_term, mixer_term, tap_term, back_gated = mixer_backward(
        team, core, back, mixer_stored, gains[0], mixer_weights, taps
    )
    mixer_part = summed_rows(team, mixer_term)
    gated_done = zero(back_gated)
    second_total = every_seat(second_team, jnp.concatenate(second_part[::-1], axis=-1), gated_done)
    attend_total = every_seat(team, attend_part, gated_done)
    first_total = every_seat(first_team, jnp.concatenate(first_part[::-1], axis=-1))
    mixer_total = every_seat(team, mixer_part)

    small = jnp.concatenate(
        [mixer_gain_term, first_gain_term, attend_gain_term, second_gain_term, scale_terms[0], scale_terms[1]]
    )
    small = small + swap_core(small)
    tap_full = lax.dynamic_update_slice_in_dim(
        jnp.zeros((3, mixer_taps.shape[1]), f32), tap_term, team.seat * channels, 1
    )
    small = grid_total(jnp.concatenate([small, tap_full.reshape(-1)]))
    gain_totals = lax.dynamic_slice_in_dim(
        small[: 4 * model].reshape(4, model), rank * gain_rows, gain_rows, 1
    )
    scale_totals = small[4 * model : 4 * model + 2 * HD].reshape(2, HD)
    tap_total = small[4 * model + 2 * HD :].reshape(tap_full.shape)

    def both_cores(own):
        return true_order(core, 1, [own, swap_core(own)])

    def joined_lift(total):
        width = total.shape[-1] // 3
        return jnp.stack([joined_hidden(units, total[..., k * width : (k + 1) * width]) for k in range(2)], axis=1)

    def joined_drop(total):
        return joined_hidden(units, total[..., 2 * total.shape[-1] // 3 :])

    rows = mixer_in.shape[0]
    in_columns = 3 * channels
    inner = attend_total.shape[-1] - query_weight.shape[1] // 4
    queries = query_weight.shape[1] // 4
    return (
        both_cores(result.astype(bf16)),
        both_cores(back),
        gain_totals[0],
        all_seats(mixer_total[..., :in_columns].reshape(4, rows, 3, channels)),
        tap_total,
        all_seats(mixer_total[..., in_columns:]),
        gain_totals[1],
        joined_lift(first_total),
        joined_drop(first_total),
        gain_totals[2],
        all_seats(attend_total[..., :queries]),
        all_seats(attend_total[..., queries:inner].reshape(4, rows, 2, -1)),
        scale_totals[0],
        scale_totals[1],
        all_seats(attend_total[..., inner:]),
        gain_totals[3],
        joined_lift(second_total),
        joined_drop(second_total),
    )


def solution(mesh):
    grid = ("dp", "seq")
    return jax.shard_map(
        body,
        mesh=mesh,
        in_specs=(
            P("dp", "seq", None),
            P("dp", "seq"),
            P(grid),
            P(grid, None, "mp"),
            P(None, "mp"),
            P(grid, "mp"),
            P(grid),
            P(grid, None, "mp"),
            P(grid, "mp"),
            P(grid),
            P(grid, "mp"),
            P(grid, None, "mp"),
            P(),
            P(),
            P(grid, "mp"),
            P(grid),
            P(grid, None, "mp"),
            P(grid, "mp"),
            P("dp", "seq", None),
        ),
        out_specs=(
            P("dp", "seq", None),
            P("dp", "seq", None),
            P(grid),
            P(grid, None, "mp"),
            P(None, "mp"),
            P(grid, "mp"),
            P(grid),
            P(grid, None, "mp"),
            P(grid, "mp"),
            P(grid),
            P(grid, "mp"),
            P(grid, None, "mp"),
            P(),
            P(),
            P(grid, "mp"),
            P(grid),
            P(grid, None, "mp"),
            P(grid, "mp"),
        ),
        check_vma=False,
    )
```

```python
import jax
import jax.numpy as jnp
from jax import lax
from jax.experimental import pallas as pl
from jax.experimental.pallas import tpu as pltpu
from jax.sharding import PartitionSpec as P

HD = 64

epsilon = 1e-05
rope_base = 1000000.0
bf16 = jnp.bfloat16
f32 = jnp.float32


def rms_scale(values):
    return lax.rsqrt(jnp.mean(values * values, axis=-1, keepdims=True) + epsilon)


def norm_back(back_normed, normed, inverse):
    return inverse * (back_normed - normed * jnp.mean(back_normed * normed, axis=-1, keepdims=True))


def frequencies():
    exponent = jnp.arange(HD // 2, dtype=f32) * (2.0 / HD)
    return jnp.power(rope_base, -exponent)


def rotate(values, cosines, sine_table):
    middle = values.shape[-1] // 2
    leading = values[..., :middle]
    trailing = values[..., middle:]
    return jnp.concatenate(
        [leading * cosines - trailing * sine_table, trailing * cosines + leading * sine_table],
        axis=-1,
    )


def dot(pattern, first, second):
    return jnp.einsum(pattern, first, second, preferred_element_type=f32)


class Team:
    def __init__(self, axis):
        self.axis = axis
        self.across = "seq" if axis == "dp" else "dp"
        self.size = lax.axis_size(axis)
        self.seat = lax.axis_index(axis)


def swap(array, axis, mask):
    return lax.ppermute(array, axis, [(i, i ^ mask) for i in range(lax.axis_size(axis))])


def swap_core(array):
    return swap(array, "mp", 1)


def shift(array, by):
    count = lax.axis_size("seq")
    return lax.ppermute(array, "seq", [(i, i + by) for i in range(count) if 0 <= i + by < count])


def zero(token):
    element = token[(0,) * token.ndim].astype(f32)
    return (element * 0.0).astype(jnp.int32)


def take(array, index, axis):
    return lax.dynamic_index_in_dim(array, index, axis, keepdims=False)


def gather_tokens(team, own):
    mine = jnp.concatenate([own] + [swap(own, team.axis, mask) for mask in range(1, team.size)], axis=0)
    return mine, swap_core(mine)


def scatter_begin(team, mine, other):
    received = swap_core(other.astype(bf16)).astype(f32)
    rows = mine.shape[0] // team.size
    both = mine + received
    sends = [(mask, both[mask * rows : (mask + 1) * rows].astype(bf16)) for mask in range(team.size - 1, 0, -1)]
    return both[:rows], sends


def scatter_end(team, total, sends):
    received = [swap(send, team.axis, mask) for mask, send in sends]
    for array in received:
        total = total + array.astype(f32)
    return total


def scatter_tokens(team, mine, other):
    total, sends = scatter_begin(team, mine, other)
    return scatter_end(team, total, sends), sends[-1][1]


def true_order(core, sequences, halves):
    mine, other = (half.reshape(sequences, -1, half.shape[-1]) for half in halves)
    return jnp.where(
        core == 0, jnp.concatenate([mine, other], axis=1), jnp.concatenate([other, mine], axis=1)
    )


def own_halves(core, ordered):
    rows = ordered.shape[1] // 2
    return [
        lax.dynamic_slice_in_dim(ordered, at * rows, rows, 1).reshape(-1, ordered.shape[-1])
        for at in (core, 1 - core)
    ]


def team_rows(team, piece_of):
    return [
        swap(piece_of(team.seat ^ mask), team.axis, mask) if mask else piece_of(team.seat)
        for mask in range(team.size)
    ]


def all_rows(team, pieces, late=0):
    lead, (rows, columns) = pieces[0].shape[:-2], pieces[0].shape[-2:]
    plain = (0,) * len(lead)
    near = jnp.zeros(lead + (team.size, rows, columns), pieces[0].dtype)
    for mask, piece in enumerate(pieces):
        near = lax.dynamic_update_slice(
            near, jnp.expand_dims(piece, len(lead)), plain + ((team.seat ^ mask) + late, 0, 0)
        )
    if team.axis == "dp":
        whole = lax.all_gather(near, team.across, axis=len(lead) + 1, tiled=True)
    else:
        near = near.reshape(lead + (team.size * rows, columns))
        whole = lax.all_gather(near, team.across, axis=len(lead), tiled=True)
    return whole.reshape(lead + (-1, columns))


def summed_rows(team, gradient):
    columns = gradient.shape[-1]
    teams = lax.axis_size(team.across)
    if team.axis == "dp":
        split = gradient.reshape(team.size, teams, -1, columns).swapaxes(0, 1)
    else:
        split = gradient.reshape(teams, team.size, -1, columns)
    rows = split.shape[2]
    part = lax.psum_scatter(split.reshape(-1, columns), team.across, scatter_dimension=0, tiled=True)
    return part.reshape(team.size, rows, columns)


def every_seat(team, part, late=0):
    axis = part.ndim - 3
    pieces = []
    for mask in range(team.size):
        piece = take(part, (team.seat ^ mask) + late, axis)
        pieces.append(swap(piece, team.axis, mask) if mask else piece)
    seats = jnp.stack(pieces)
    shape, bits = seats.shape, team.size.bit_length() - 1
    seats = seats.reshape((2,) * bits + shape[1:])
    for bit in range(bits):
        seats = jnp.where((team.seat >> bit) & 1 == 1, jnp.flip(seats, bits - 1 - bit), seats)
    return seats.reshape(shape).astype(f32)


def hidden_width(units, seats):
    tiles = -(-units // (128 * seats))
    return tiles * 128 if units % 128 == 0 else units // seats


def hidden_start(units, seats, seat):
    width = hidden_width(units, seats)
    return jnp.minimum(seat * width, units - width)


def hidden_mask(units, seats, seat):
    width = hidden_width(units, seats)
    doubled = seat * width - hidden_start(units, seats, seat)
    return (lax.broadcasted_iota(jnp.int32, (1, width), 1) >= doubled).astype(f32)


def joined_hidden(units, pieces):
    seats = len(pieces)
    width = hidden_width(units, seats)
    parts = []
    for seat in range(seats):
        low, start = seat * width, min(seat * width, units - width)
        if low < units:
            parts.append(pieces[seat][..., low - start : min(low + width, units) - start])
    return jnp.concatenate(parts, axis=-1)


def quarter(array, seat):
    width = array.shape[-1] // 4
    return array[..., seat * width : (seat + 1) * width]


def all_seats(array):
    return jnp.concatenate([array[i] for i in range(4)], axis=-1)


def pack_mixer(weight_in, weight_out):
    seats = [
        jnp.concatenate([quarter(weight_in[:, k], i) for k in range(3)] + [quarter(weight_out, i)], axis=-1)
        for i in range(4)
    ]
    return jnp.stack(seats)


def pack_attend(query_weight, pair_weight, out_weight):
    seats = [
        jnp.concatenate(
            [quarter(query_weight, i)]
            + [quarter(pair_weight[:, k], i) for k in range(2)]
            + [quarter(out_weight, i)],
            axis=-1,
        )
        for i in range(4)
    ]
    return jnp.stack(seats)


def lowered_norm(hidden, gain):
    inverse = rms_scale(hidden)
    normed = hidden * inverse
    return inverse, normed, (normed * gain).astype(bf16)


def after_norm(back_out, back_normed, normed, inverse, gain):
    gain_term = jnp.sum(back_normed * normed, axis=0)
    return back_out + norm_back(back_normed * gain, normed, inverse), gain_term


def project(pattern, halves, weights):
    return [dot(pattern, half, weights) for half in halves]


def project_out(team, pattern, halves, weights):
    other = dot(pattern, halves[1], weights)
    mine = dot(pattern, halves[0], weights)
    return scatter_tokens(team, mine, other)


def outer(first, second):
    return (dot("td,tf->df", first[0], second[0]) + dot("td,tf->df", first[1], second[1])).astype(bf16)


def feed_active(tokens, lift, mask):
    both = dot("td,df->tf", tokens, lift)
    width = both.shape[1] // 2
    gate, up = both[:, :width], both[:, width:]
    return gate, up, (jax.nn.silu(gate) * up * mask).astype(bf16)


def feed_back(back_tokens, gate, up, drop, mask):
    back_active = dot("td,df->tf", back_tokens, drop) * mask
    sigmoid_value = jax.nn.sigmoid(gate)
    back_gate = back_active * up * sigmoid_value * (1.0 + gate * (1.0 - sigmoid_value))
    return jnp.concatenate([back_gate, back_active * gate * sigmoid_value], axis=1).astype(bf16)


def feed_forward(team, hidden, gain, lift, mask):
    inverse, normed, lowered = lowered_norm(hidden, gain)
    tokens = gather_tokens(team, lowered)
    gate, up, active = zip(*[feed_active(half, lift, mask) for half in tokens])
    return inverse, normed, tokens, gate, up, active


def held(array, token):
    return array + zero(token).astype(array.dtype)


def feed_backward(team, back_out, back_tokens, stored, gain, lift, drop, mask, hold):
    inverse, normed, tokens, gate, up, active = stored
    back_pair = [feed_back(back_tokens[i], gate[i], up[i], drop, mask) for i in range(2)]
    back_normed, sent = project_out(team, "tf,df->td", back_pair, lift)
    drop_part = summed_rows(team, outer(back_tokens, active))
    if hold is None:
        back_pair = [held(half, sent) for half in back_pair]
    lift_part = summed_rows(team, outer(tokens, back_pair))
    if hold is not None:
        gain = held(held(gain, drop_part), hold)
    back_hidden, gain_term = after_norm(back_out, back_normed, normed, inverse, gain)
    return back_hidden, gain_term, drop_part, lift_part


def mixer_forward(team, core, hidden, token_halves, order, gain, weights, taps):
    inverse = rms_scale(hidden)
    normed = hidden * inverse
    tokens = [lowered_norm(half.astype(f32), gain)[2] for half in token_halves]
    channels = taps.shape[1]
    parts = true_order(core, team.size, project("td,dc->tc", tokens, weights[:, : 3 * channels]))
    gate_in, gate_out, value = (parts[..., i * channels : (i + 1) * channels] for i in range(3))
    mixed = (gate_in * value).astype(bf16)
    earlier = shift(mixed[:, -2:], 1)
    padded = jnp.concatenate([earlier, mixed], axis=1).astype(f32)
    one_back = (order >= 1).astype(f32)[..., None]
    two_back = (order >= 2).astype(f32)[..., None]
    convolved = (
        taps[2] * padded[:, 2:] + taps[1] * padded[:, 1:-1] * one_back + taps[0] * padded[:, :-2] * two_back
    )
    gated = own_halves(core, (gate_out * convolved).astype(bf16))
    out, sent = project_out(team, "tc,dc->td", gated, weights[:, 3 * channels :])
    stored = (inverse, normed, tokens, gate_in, gate_out, value, padded, convolved, gated, one_back, two_back)
    return hidden + out, stored, parts


def mixer_backward(team, core, back_out, stored, gain, weights, taps):
    inverse, normed, tokens, gate_in, gate_out, value, padded, convolved, gated, one_back, two_back = stored
    channels = taps.shape[1]
    back_tokens = gather_tokens(team, back_out.astype(bf16))
    back_gated = true_order(core, team.size, project("td,dc->tc", back_tokens, weights[:, 3 * channels :]))
    back_conv = back_gated * gate_out
    back_padded = (
        jnp.pad(taps[2] * back_conv, ((0, 0), (2, 0), (0, 0)))
        + jnp.pad(taps[1] * back_conv * one_back, ((0, 0), (1, 1), (0, 0)))
        + jnp.pad(taps[0] * back_conv * two_back, ((0, 0), (0, 2), (0, 0)))
    )
    later = shift(back_padded[:, :2], -1)
    back_mixed = back_padded[:, 2:] + jnp.pad(later, ((0, 0), (back_conv.shape[1] - 2, 0), (0, 0)))
    back_parts = own_halves(
        core,
        jnp.concatenate(
            [back_mixed * value, back_gated * convolved, back_mixed * gate_in], axis=-1
        ).astype(bf16),
    )
    back_normed, sent = project_out(team, "tc,dc->td", back_parts, weights[:, : 3 * channels])
    tap_term = jnp.stack(
        [
            jnp.sum(back_conv * padded[:, :-2] * two_back, axis=(0, 1)),
            jnp.sum(back_conv * padded[:, 1:-1] * one_back, axis=(0, 1)),
            jnp.sum(back_conv * padded[:, 2:], axis=(0, 1)),
        ]
    )
    term = jnp.concatenate([outer(tokens, back_parts), outer(back_tokens, gated)], axis=-1)
    back_hidden, gain_term = after_norm(back_out, back_normed, normed, inverse, gain)
    return back_hidden, gain_term, term, tap_term, back_gated


def turned(first, second):
    return lax.dot_general(first, second, (((1,), (1,)), ((), ())), preferred_element_type=f32)


def summed(first, second):
    return lax.dot_general(first, second, (((0,), (0,)), ((), ())), preferred_element_type=f32)


def allowed_keys(base_ref, order_ref, keys, count):
    base = base_ref[0]
    slot_row = lax.broadcasted_iota(jnp.int32, (keys, 1), 0)
    slot = lax.div(slot_row, count)
    key_index = base + slot_row - 2 * slot * count
    query_index = base + lax.broadcasted_iota(jnp.int32, (1, count), 1)
    return (key_index <= query_index) & (key_index >= query_index - order_ref[0])


def key_probs(query, keys, allowed):
    scores = jnp.where(allowed, turned(keys, query) * HD**-0.5, -1e30)
    weights = jnp.exp(scores - jnp.max(scores, axis=0, keepdims=True))
    return weights * (1.0 / jnp.sum(weights, axis=0, keepdims=True))


def attend_kernel(base_ref, order_ref, query_ref, slots_ref, out_ref):
    count, keys = query_ref.shape[1], slots_ref.shape[1]
    allowed = allowed_keys(base_ref, order_ref, keys, count)
    key, value = slots_ref[0, :, :HD], slots_ref[0, :, HD:]
    parts = []
    for head in range(query_ref.shape[2] // HD):
        query = query_ref[0, :, head * HD : (head + 1) * HD]
        probs = key_probs(query, key, allowed)
        parts.append(summed(probs.astype(bf16), value))
    out_ref[0] = jnp.concatenate(parts, axis=1).astype(bf16)


def attend_back_kernel(base_ref, order_ref, query_ref, back_ref, slots_ref, back_query_ref, own_ref, rest_ref):
    count, keys = query_ref.shape[1], slots_ref.shape[1]
    allowed = allowed_keys(base_ref, order_ref, keys, count)
    key, value = slots_ref[0, :, :HD], slots_ref[0, :, HD:]
    back_queries = []
    back_key = jnp.zeros((keys, HD), f32)
    back_value = jnp.zeros((keys, HD), f32)
    for head in range(query_ref.shape[2] // HD):
        query = query_ref[0, :, head * HD : (head + 1) * HD]
        back = back_ref[0, :, head * HD : (head + 1) * HD]
        probs = key_probs(query, key, allowed)
        back_probs = turned(value, back)
        row_dot = jnp.sum(probs * back_probs, axis=0, keepdims=True)
        back_scores = (probs * (back_probs - row_dot)).astype(bf16)
        back_queries.append(summed(back_scores, key) * HD**-0.5)
        back_key += jnp.dot(back_scores, query, preferred_element_type=f32)
        back_value += jnp.dot(probs.astype(bf16), back, preferred_element_type=f32)
    back_query_ref[0] = jnp.concatenate(back_queries, axis=1)
    back_pair = jnp.concatenate([back_key * HD**-0.5, back_value], axis=1)
    own_ref[0] = back_pair[:count]
    rest_ref[0] = back_pair[count:].astype(bf16)


def attend_call(kernel, base, order, arrays, outs):
    sequences, count = order.shape

    def block(shape):
        return pl.BlockSpec((1,) + tuple(shape[1:]), lambda i: (i, 0, 0))

    keys = arrays[-1].shape[1]
    heads = arrays[0].shape[2] // HD
    return pl.pallas_call(
        kernel,
        grid=(sequences,),
        in_specs=[pl.BlockSpec(memory_space=pltpu.SMEM), block((sequences, 1, count))]
        + [block(array.shape) for array in arrays],
        out_specs=[block(out.shape) for out in outs],
        out_shape=outs,
        compiler_params=pltpu.CompilerParams(vmem_limit_bytes=56 * 1024 * 1024),
        cost_estimate=pl.CostEstimate(
            flops=10 * sequences * heads * count * keys * HD,
            bytes_accessed=sum(2 * array.size for array in arrays),
            transcendentals=sequences * heads * count * keys,
        ),
    )(base.reshape(1), order.reshape(sequences, 1, count), *arrays)


def attend_forward(team, core, hidden, order, gain, weights, query_gain, key_gain):
    inverse, normed, lowered = lowered_norm(hidden, gain)
    tokens = gather_tokens(team, lowered)
    heads = weights.shape[1] * 3 // 8 // HD
    groups = weights.shape[1] // 8 // HD
    repeat = heads // groups
    inner = (heads + 2 * groups) * HD
    mixed = true_order(core, team.size, project("td,dc->tc", tokens, weights[:, :inner]))
    sequences, count = mixed.shape[:2]
    query_heads = mixed[..., : heads * HD].reshape(sequences, count, heads, HD)
    key_heads = mixed[..., heads * HD : (heads + groups) * HD].reshape(sequences, count, groups, HD)
    value_low = mixed[..., (heads + groups) * HD :].astype(bf16)
    angles = order.astype(f32)[..., None] * frequencies()
    cosines, sines = jnp.cos(angles)[:, :, None, :], jnp.sin(angles)[:, :, None, :]
    query_inverse = rms_scale(query_heads)
    query_normed = query_heads * query_inverse
    query_rot = rotate(query_normed * query_gain, cosines, sines).astype(bf16)
    key_inverse = rms_scale(key_heads)
    key_normed = key_heads * key_inverse
    key_rot = rotate(key_normed * key_gain, cosines, sines).astype(bf16)
    pair = jnp.concatenate([key_rot.reshape(sequences, count, groups * HD), value_low], axis=-1)
    blocks = lax.axis_size("seq")
    here = lax.axis_index("seq")
    slots = jnp.concatenate([shift(pair, i) if i else pair for i in range(blocks)], axis=1)
    base = (here * count).astype(jnp.int32)
    query_rot = query_rot.reshape(sequences, count, heads * HD)
    (attended,) = attend_call(
        attend_kernel, base, order, [query_rot, slots], [jax.ShapeDtypeStruct((sequences, count, heads * HD), bf16)]
    )
    attended = own_halves(core, attended)
    out, sent = project_out(team, "tc,dc->td", attended, weights[:, inner:])
    stored = (
        inverse,
        normed,
        tokens,
        query_inverse,
        query_normed,
        key_inverse,
        key_normed,
        cosines,
        sines,
        query_rot,
        slots,
        base,
        order,
        attended,
    )
    return hidden + out, stored, mixed


def attend_backward(team, core, back_out, stored, gain, weights, query_gain, key_gain, before):
    (
        inverse,
        normed,
        tokens,
        query_inverse,
        query_normed,
        key_inverse,
        key_normed,
        cosines,
        sines,
        query_rot,
        slots,
        base,
        order,
        attended,
    ) = stored
    sequences, count = query_rot.shape[:2]
    heads, groups = query_rot.shape[2] // HD, slots.shape[2] // (2 * HD)
    inner = (heads + 2 * groups) * HD
    back_tokens = gather_tokens(team, back_out.astype(bf16))
    back_attended = true_order(core, team.size, project("td,dc->tc", back_tokens, held(weights[:, inner:], before[0]))).astype(bf16)
    back_query_rot, back_pair, rest = attend_call(
        attend_back_kernel,
        base,
        order,
        [query_rot, back_attended, slots],
        [
            jax.ShapeDtypeStruct((sequences, count, heads * HD), f32),
            jax.ShapeDtypeStruct((sequences, count, 2 * HD), f32),
            jax.ShapeDtypeStruct((sequences, slots.shape[1] - count, 2 * HD), bf16),
        ],
    )
    for i in range(1, slots.shape[1] // count):
        back_pair = back_pair + shift(rest[:, (i - 1) * count : i * count], -i).astype(f32)
    back_query_scaled = rotate(back_query_rot.reshape(sequences, count, heads, HD), cosines, -sines)
    query_scale_term = jnp.sum(back_query_scaled * query_normed, axis=(0, 1, 2))
    back_query = norm_back(back_query_scaled * query_gain, query_normed, query_inverse)
    back_key_rot = back_pair[..., : groups * HD].reshape(sequences, count, groups, HD)
    back_key_scaled = rotate(back_key_rot, cosines, -sines)
    key_scale_term = jnp.sum(back_key_scaled * key_normed, axis=(0, 1, 2))
    back_key = norm_back(back_key_scaled * key_gain, key_normed, key_inverse)
    back_mixed = jnp.concatenate(
        [
            back_query.reshape(sequences, count, heads * HD),
            back_key.reshape(sequences, count, groups * HD),
            back_pair[..., groups * HD :],
        ],
        axis=-1,
    ).astype(bf16)
    back_mixed = own_halves(core, back_mixed)
    back_normed, sent = project_out(team, "tc,dc->td", back_mixed, held(weights[:, :inner], before[1]))
    term = jnp.concatenate([outer(tokens, back_mixed), outer(back_tokens, attended)], axis=-1)
    back_hidden, gain_term = after_norm(back_out, back_normed, normed, inverse, gain)
    return back_hidden, gain_term, term, (query_scale_term, key_scale_term), back_attended


def grid_total(array):
    for axis in ("dp", "seq"):
        mask = 1
        while mask < lax.axis_size(axis):
            array = array + swap(array, axis, mask)
            mask *= 2
    return array


def body(
    hidden_in,
    positions,
    mixer_gain,
    mixer_in,
    mixer_taps,
    mixer_out,
    first_gain,
    first_lift,
    first_drop,
    attend_gain,
    query_weight,
    pair_weight,
    query_scale,
    key_scale,
    attend_out,
    second_gain,
    second_lift,
    second_drop,
    cotangent,
):
    core = lax.axis_index("mp")
    team = Team("dp")
    first_team = second_team = team
    rank = lax.axis_index("dp") * lax.axis_size("seq") + lax.axis_index("seq")
    model = hidden_in.shape[-1]
    share = hidden_in.shape[1] // 2
    own_tokens = lax.dynamic_slice_in_dim(hidden_in[0], core * share, share)
    hidden = own_tokens.astype(f32)
    signal_low = lax.dynamic_slice_in_dim(cotangent[0], core * share, share)
    signal = signal_low.astype(f32)
    query_gain, key_gain = query_scale.astype(f32), key_scale.astype(f32)
    channels = mixer_taps.shape[1] // team.size
    taps = lax.dynamic_slice_in_dim(mixer_taps, team.seat * channels, channels, 1).astype(f32)
    units = first_drop.shape[1]
    first_mask = hidden_mask(units, first_team.size, first_team.seat)
    second_mask = hidden_mask(units, second_team.size, second_team.seat)

    def feed_piece(on, lift, drop, late):
        width = hidden_width(units, on.size)

        def piece(seat):
            start = hidden_start(units, on.size, seat) + late
            parts = [lift[:, 0], lift[:, 1], drop]
            return jnp.concatenate([lax.dynamic_slice_in_dim(part, start, width, 1) for part in parts], axis=1)

        return piece

    def lift_of(pieces):
        return [piece[:, : 2 * piece.shape[1] // 3] for piece in pieces]

    def drop_of(pieces):
        return [piece[:, 2 * piece.shape[1] // 3 :] for piece in pieces]

    token_halves = gather_tokens(team, own_tokens)
    packed = pack_mixer(mixer_in, mixer_out)
    got = team_rows(team, lambda seat: take(packed, seat, 0))
    mixer_weights = all_rows(team, got)
    near_done = zero(got[-1])

    got_first = team_rows(first_team, feed_piece(first_team, first_lift, first_drop, near_done))
    first_lift_all = all_rows(first_team, lift_of(got_first))
    first_drop_all = all_rows(first_team, drop_of(got_first))
    near_done = zero(got_first[-1])

    gain_rows = mixer_gain.shape[0]
    gains = jnp.stack([mixer_gain, first_gain, attend_gain, second_gain]).astype(f32)
    gains = grid_total(
        lax.dynamic_update_slice_in_dim(jnp.zeros((4, model), f32), gains, rank * gain_rows + near_done, 1)
    )
    own_places = positions[0] + near_done
    order = jnp.stack([own_places] + [swap(own_places, team.axis, mask) for mask in range(1, team.size)])

    packed_attend = pack_attend(query_weight, pair_weight, attend_out)
    got_attend = team_rows(team, lambda seat: take(packed_attend, seat + near_done, 0))
    got_second = team_rows(second_team, feed_piece(second_team, second_lift, second_drop, near_done))

    after_mixer, mixer_stored, parts = mixer_forward(
        team, core, hidden, token_halves, order, gains[0], mixer_weights, taps
    )
    mixed_done = zero(parts)
    beside = [jnp.concatenate(pair, axis=1) for pair in zip(got_attend, drop_of(got_second))]
    shared = all_rows(team, beside, mixed_done)
    attend_weights, second_drop_all = shared[:, : got_attend[0].shape[1]], shared[:, got_attend[0].shape[1] :]
    second_lift_all = all_rows(second_team, lift_of(got_second), mixed_done)

    first_stored = feed_forward(first_team, after_mixer, gains[1], first_lift_all, first_mask)
    out, sent = project_out(first_team, "tf,df->td", first_stored[-1], first_drop_all)
    after_first = after_mixer + out
    after_attend, attend_stored, mixed = attend_forward(
        team, core, after_first, order, gains[2], attend_weights, query_gain, key_gain
    )
    signal_low = signal_low + zero(mixed).astype(bf16)
    signal_tokens = gather_tokens(second_team, signal_low)
    second_stored = feed_forward(second_team, after_attend, gains[3], second_lift_all, second_mask)

    result_sums, result_sends = scatter_begin(
        second_team, *project("tf,df->td", second_stored[-1], second_drop_all)
    )
    second_mask = held(second_mask, result_sends[-1][1])

    back, second_gain_term, *second_part = feed_backward(
        second_team, signal, signal_tokens, second_stored, gains[3], second_lift_all, second_drop_all, second_mask, None
    )
    back, attend_gain_term, attend_term, scale_terms, back_attended = attend_backward(
        team, core, back, attend_stored, gains[2], attend_weights, query_gain, key_gain, second_part
    )
    attend_part = summed_rows(team, attend_term)
    result = after_attend + scatter_end(second_team, held(result_sums, back_attended), result_sends)

    first_back_tokens = gather_tokens(first_team, back.astype(bf16))
    back, first_gain_term, *first_part = feed_backward(
        first_team, back, first_back_tokens, first_stored, gains[1], first_lift_all, first_drop_all, first_mask, attend_part
    )
    back, mixer_gain_term, mixer_term, tap_term, back_gated = mixer_backward(
        team, core, back, mixer_stored, gains[0], mixer_weights, taps
    )
    mixer_part = summed_rows(team, mixer_term)
    gated_done = zero(back_gated)
    second_total = every_seat(second_team, jnp.concatenate(second_part[::-1], axis=-1), gated_done)
    attend_total = every_seat(team, attend_part, gated_done)
    first_total = every_seat(first_team, jnp.concatenate(first_part[::-1], axis=-1))
    mixer_total = every_seat(team, mixer_part)

    small = jnp.concatenate(
        [mixer_gain_term, first_gain_term, attend_gain_term, second_gain_term, scale_terms[0], scale_terms[1]]
    )
    small = small + swap_core(small)
    tap_full = lax.dynamic_update_slice_in_dim(
        jnp.zeros((3, mixer_taps.shape[1]), f32), tap_term, team.seat * channels, 1
    )
    small = grid_total(jnp.concatenate([small, tap_full.reshape(-1)]))
    gain_totals = lax.dynamic_slice_in_dim(
        small[: 4 * model].reshape(4, model), rank * gain_rows, gain_rows, 1
    )
    scale_totals = small[4 * model : 4 * model + 2 * HD].reshape(2, HD)
    tap_total = small[4 * model + 2 * HD :].reshape(tap_full.shape)

    def both_cores(own):
        return true_order(core, 1, [own, swap_core(own)])

    def joined_lift(total):
        width = total.shape[-1] // 3
        return jnp.stack([joined_hidden(units, total[..., k * width : (k + 1) * width]) for k in range(2)], axis=1)

    def joined_drop(total):
        return joined_hidden(units, total[..., 2 * total.shape[-1] // 3 :])

    rows = mixer_in.shape[0]
    in_columns = 3 * channels
    inner = attend_total.shape[-1] - query_weight.shape[1] // 4
    queries = query_weight.shape[1] // 4
    return (
        both_cores(result.astype(bf16)),
        both_cores(back),
        gain_totals[0],
        all_seats(mixer_total[..., :in_columns].reshape(4, rows, 3, channels)),
        tap_total,
        all_seats(mixer_total[..., in_columns:]),
        gain_totals[1],
        joined_lift(first_total),
        joined_drop(first_total),
        gain_totals[2],
        all_seats(attend_total[..., :queries]),
        all_seats(attend_total[..., queries:inner].reshape(4, rows, 2, -1)),
        scale_totals[0],
        scale_totals[1],
        all_seats(attend_total[..., inner:]),
        gain_totals[3],
        joined_lift(second_total),
        joined_drop(second_total),
    )


def solution(mesh):
    grid = ("dp", "seq")
    return jax.shard_map(
        body,
        mesh=mesh,
        in_specs=(
            P("dp", "seq", None),
            P("dp", "seq"),
            P(grid),
            P(grid, None, "mp"),
            P(None, "mp"),
            P(grid, "mp"),
            P(grid),
            P(grid, None, "mp"),
            P(grid, "mp"),
            P(grid),
            P(grid, "mp"),
            P(grid, None, "mp"),
            P(),
            P(),
            P(grid, "mp"),
            P(grid),
            P(grid, None, "mp"),
            P(grid, "mp"),
            P("dp", "seq", None),
        ),
        out_specs=(
            P("dp", "seq", None),
            P("dp", "seq", None),
            P(grid),
            P(grid, None, "mp"),
            P(None, "mp"),
            P(grid, "mp"),
            P(grid),
            P(grid, None, "mp"),
            P(grid, "mp"),
            P(grid),
            P(grid, "mp"),
            P(grid, None, "mp"),
            P(),
            P(),
            P(grid, "mp"),
            P(grid),
            P(grid, None, "mp"),
            P(grid, "mp"),
        ),
        check_vma=False,
    )
```

```python
import jax
import jax.numpy as jnp
from jax import lax
from jax.experimental import pallas as pl
from jax.experimental.pallas import tpu as pltpu
from jax.sharding import PartitionSpec as P

HD = 64

epsilon = 1e-05
rope_base = 1000000.0
bf16 = jnp.bfloat16
f32 = jnp.float32


def rms_scale(values):
    return lax.rsqrt(jnp.mean(values * values, axis=-1, keepdims=True) + epsilon)


def norm_back(back_normed, normed, inverse):
    return inverse * (back_normed - normed * jnp.mean(back_normed * normed, axis=-1, keepdims=True))


def frequencies():
    exponent = jnp.arange(HD // 2, dtype=f32) * (2.0 / HD)
    return jnp.power(rope_base, -exponent)


def rotate(values, cosines, sine_table):
    middle = values.shape[-1] // 2
    leading = values[..., :middle]
    trailing = values[..., middle:]
    return jnp.concatenate(
        [leading * cosines - trailing * sine_table, trailing * cosines + leading * sine_table],
        axis=-1,
    )


def dot(pattern, first, second):
    return jnp.einsum(pattern, first, second, preferred_element_type=f32)


class Team:
    def __init__(self, axis):
        self.axis = axis
        self.across = "seq" if axis == "dp" else "dp"
        self.size = lax.axis_size(axis)
        self.seat = lax.axis_index(axis)


def swap(array, axis, mask):
    return lax.ppermute(array, axis, [(i, i ^ mask) for i in range(lax.axis_size(axis))])


def swap_core(array):
    return swap(array, "mp", 1)


def shift(array, by):
    count = lax.axis_size("seq")
    return lax.ppermute(array, "seq", [(i, i + by) for i in range(count) if 0 <= i + by < count])


def zero(token):
    element = token[(0,) * token.ndim].astype(f32)
    return (element * 0.0).astype(jnp.int32)


def take(array, index, axis):
    return lax.dynamic_index_in_dim(array, index, axis, keepdims=False)


def gather_tokens(team, own):
    mine = jnp.concatenate([own] + [swap(own, team.axis, mask) for mask in range(1, team.size)], axis=0)
    return mine, swap_core(mine)


def scatter_begin(team, mine, other):
    received = swap_core(other.astype(bf16)).astype(f32)
    rows = mine.shape[0] // team.size
    both = mine + received
    sends = [(mask, both[mask * rows : (mask + 1) * rows].astype(bf16)) for mask in range(team.size - 1, 0, -1)]
    return both[:rows], sends


def scatter_end(team, total, sends):
    received = [swap(send, team.axis, mask) for mask, send in sends]
    for array in received:
        total = total + array.astype(f32)
    return total


def scatter_tokens(team, mine, other):
    total, sends = scatter_begin(team, mine, other)
    return scatter_end(team, total, sends), sends[-1][1]


def true_order(core, sequences, halves):
    mine, other = (half.reshape(sequences, -1, half.shape[-1]) for half in halves)
    return jnp.where(
        core == 0, jnp.concatenate([mine, other], axis=1), jnp.concatenate([other, mine], axis=1)
    )


def own_halves(core, ordered):
    rows = ordered.shape[1] // 2
    return [
        lax.dynamic_slice_in_dim(ordered, at * rows, rows, 1).reshape(-1, ordered.shape[-1])
        for at in (core, 1 - core)
    ]


def team_rows(team, piece_of):
    return [
        swap(piece_of(team.seat ^ mask), team.axis, mask) if mask else piece_of(team.seat)
        for mask in range(team.size)
    ]


def all_rows(team, pieces, late=0):
    lead, (rows, columns) = pieces[0].shape[:-2], pieces[0].shape[-2:]
    plain = (0,) * len(lead)
    near = jnp.zeros(lead + (team.size, rows, columns), pieces[0].dtype)
    for mask, piece in enumerate(pieces):
        near = lax.dynamic_update_slice(
            near, jnp.expand_dims(piece, len(lead)), plain + ((team.seat ^ mask) + late, 0, 0)
        )
    if team.axis == "dp":
        whole = lax.all_gather(near, team.across, axis=len(lead) + 1, tiled=True)
    else:
        near = near.reshape(lead + (team.size * rows, columns))
        whole = lax.all_gather(near, team.across, axis=len(lead), tiled=True)
    return whole.reshape(lead + (-1, columns))


def summed_rows(team, gradient):
    columns = gradient.shape[-1]
    teams = lax.axis_size(team.across)
    if team.axis == "dp":
        split = gradient.reshape(team.size, teams, -1, columns).swapaxes(0, 1)
    else:
        split = gradient.reshape(teams, team.size, -1, columns)
    rows = split.shape[2]
    part = lax.psum_scatter(split.reshape(-1, columns), team.across, scatter_dimension=0, tiled=True)
    return part.reshape(team.size, rows, columns)


def every_seat(team, part, late=0):
    axis = part.ndim - 3
    pieces = []
    for mask in range(team.size):
        piece = take(part, (team.seat ^ mask) + late, axis)
        pieces.append(swap(piece, team.axis, mask) if mask else piece)
    seats = jnp.stack(pieces)
    shape, bits = seats.shape, team.size.bit_length() - 1
    seats = seats.reshape((2,) * bits + shape[1:])
    for bit in range(bits):
        seats = jnp.where((team.seat >> bit) & 1 == 1, jnp.flip(seats, bits - 1 - bit), seats)
    return seats.reshape(shape).astype(f32)


def hidden_width(units, seats):
    tiles = -(-units // (128 * seats))
    return tiles * 128 if units % 128 == 0 else units // seats


def hidden_start(units, seats, seat):
    width = hidden_width(units, seats)
    return jnp.minimum(seat * width, units - width)


def hidden_mask(units, seats, seat):
    width = hidden_width(units, seats)
    doubled = seat * width - hidden_start(units, seats, seat)
    return (lax.broadcasted_iota(jnp.int32, (1, width), 1) >= doubled).astype(f32)


def joined_hidden(units, pieces):
    seats = len(pieces)
    width = hidden_width(units, seats)
    parts = []
    for seat in range(seats):
        low, start = seat * width, min(seat * width, units - width)
        if low < units:
            parts.append(pieces[seat][..., low - start : min(low + width, units) - start])
    return jnp.concatenate(parts, axis=-1)


def quarter(array, seat):
    width = array.shape[-1] // 4
    return array[..., seat * width : (seat + 1) * width]


def all_seats(array):
    return jnp.concatenate([array[i] for i in range(4)], axis=-1)


def pack_mixer(weight_in, weight_out):
    seats = [
        jnp.concatenate([quarter(weight_in[:, k], i) for k in range(3)] + [quarter(weight_out, i)], axis=-1)
        for i in range(4)
    ]
    return jnp.stack(seats)


def pack_attend(query_weight, pair_weight, out_weight):
    seats = [
        jnp.concatenate(
            [quarter(query_weight, i)]
            + [quarter(pair_weight[:, k], i) for k in range(2)]
            + [quarter(out_weight, i)],
            axis=-1,
        )
        for i in range(4)
    ]
    return jnp.stack(seats)


def lowered_norm(hidden, gain):
    inverse = rms_scale(hidden)
    normed = hidden * inverse
    return inverse, normed, (normed * gain).astype(bf16)


def after_norm(back_out, back_normed, normed, inverse, gain):
    gain_term = jnp.sum(back_normed * normed, axis=0)
    return back_out + norm_back(back_normed * gain, normed, inverse), gain_term


def project(pattern, halves, weights):
    return [dot(pattern, half, weights) for half in halves]


def project_out(team, pattern, halves, weights):
    other = dot(pattern, halves[1], weights)
    mine = dot(pattern, halves[0], weights)
    return scatter_tokens(team, mine, other)


def outer(first, second):
    return (dot("td,tf->df", first[0], second[0]) + dot("td,tf->df", first[1], second[1])).astype(bf16)


def feed_active(tokens, lift, mask):
    both = dot("td,df->tf", tokens, lift)
    width = both.shape[1] // 2
    gate, up = both[:, :width], both[:, width:]
    return gate, up, (jax.nn.silu(gate) * up * mask).astype(bf16)


def feed_back(back_tokens, gate, up, drop, mask):
    back_active = dot("td,df->tf", back_tokens, drop) * mask
    sigmoid_value = jax.nn.sigmoid(gate)
    back_gate = back_active * up * sigmoid_value * (1.0 + gate * (1.0 - sigmoid_value))
    return jnp.concatenate([back_gate, back_active * gate * sigmoid_value], axis=1).astype(bf16)


def feed_forward(team, hidden, gain, lift, mask):
    inverse, normed, lowered = lowered_norm(hidden, gain)
    tokens = gather_tokens(team, lowered)
    gate, up, active = zip(*[feed_active(half, lift, mask) for half in tokens])
    return inverse, normed, tokens, gate, up, active


def held(array, token):
    return array + zero(token).astype(array.dtype)


def feed_backward(team, back_out, back_tokens, stored, gain, lift, drop, mask, hold):
    inverse, normed, tokens, gate, up, active = stored
    back_pair = [feed_back(back_tokens[i], gate[i], up[i], drop, mask) for i in range(2)]
    back_normed, sent = project_out(team, "tf,df->td", back_pair, lift)
    drop_part = summed_rows(team, outer(back_tokens, active))
    lift_part = summed_rows(team, outer(tokens, back_pair))
    if hold is not None:
        gain = held(held(gain, drop_part), hold)
    back_hidden, gain_term = after_norm(back_out, back_normed, normed, inverse, gain)
    return back_hidden, gain_term, drop_part, lift_part


def mixer_forward(team, core, hidden, token_halves, order, gain, weights, taps):
    inverse = rms_scale(hidden)
    normed = hidden * inverse
    tokens = [lowered_norm(half.astype(f32), gain)[2] for half in token_halves]
    channels = taps.shape[1]
    parts = true_order(core, team.size, project("td,dc->tc", tokens, weights[:, : 3 * channels]))
    gate_in, gate_out, value = (parts[..., i * channels : (i + 1) * channels] for i in range(3))
    mixed = (gate_in * value).astype(bf16)
    earlier = shift(mixed[:, -2:], 1)
    padded = jnp.concatenate([earlier, mixed], axis=1).astype(f32)
    one_back = (order >= 1).astype(f32)[..., None]
    two_back = (order >= 2).astype(f32)[..., None]
    convolved = (
        taps[2] * padded[:, 2:] + taps[1] * padded[:, 1:-1] * one_back + taps[0] * padded[:, :-2] * two_back
    )
    gated = own_halves(core, (gate_out * convolved).astype(bf16))
    out, sent = project_out(team, "tc,dc->td", gated, weights[:, 3 * channels :])
    stored = (inverse, normed, tokens, gate_in, gate_out, value, padded, convolved, gated, one_back, two_back)
    return hidden + out, stored, parts


def mixer_backward(team, core, back_out, stored, gain, weights, taps, before):
    inverse, normed, tokens, gate_in, gate_out, value, padded, convolved, gated, one_back, two_back = stored
    channels = taps.shape[1]
    back_tokens = gather_tokens(team, back_out.astype(bf16))
    back_gated = true_order(core, team.size, project("td,dc->tc", back_tokens, weights[:, 3 * channels :]))
    back_conv = back_gated * gate_out
    back_padded = (
        jnp.pad(taps[2] * back_conv, ((0, 0), (2, 0), (0, 0)))
        + jnp.pad(taps[1] * back_conv * one_back, ((0, 0), (1, 1), (0, 0)))
        + jnp.pad(taps[0] * back_conv * two_back, ((0, 0), (0, 2), (0, 0)))
    )
    later = shift(back_padded[:, :2], -1)
    back_mixed = back_padded[:, 2:] + jnp.pad(later, ((0, 0), (back_conv.shape[1] - 2, 0), (0, 0)))
    back_parts = own_halves(
        core,
        jnp.concatenate(
            [back_mixed * value, back_gated * convolved, back_mixed * gate_in], axis=-1
        ).astype(bf16),
    )
    back_normed, sent = project_out(team, "tc,dc->td", back_parts, weights[:, : 3 * channels])
    tap_term = jnp.stack(
        [
            jnp.sum(back_conv * padded[:, :-2] * two_back, axis=(0, 1)),
            jnp.sum(back_conv * padded[:, 1:-1] * one_back, axis=(0, 1)),
            jnp.sum(back_conv * padded[:, 2:], axis=(0, 1)),
        ]
    )
    term = jnp.concatenate([outer(tokens, back_parts), outer(back_tokens, gated)], axis=-1)
    back_hidden, gain_term = after_norm(back_out, back_normed, normed, inverse, held(gain, before))
    return back_hidden, gain_term, term, tap_term, back_gated


def turned(first, second):
    return lax.dot_general(first, second, (((1,), (1,)), ((), ())), preferred_element_type=f32)


def summed(first, second):
    return lax.dot_general(first, second, (((0,), (0,)), ((), ())), preferred_element_type=f32)


def allowed_keys(base_ref, order_ref, keys, count):
    base = base_ref[0]
    slot_row = lax.broadcasted_iota(jnp.int32, (keys, 1), 0)
    slot = lax.div(slot_row, count)
    key_index = base + slot_row - 2 * slot * count
    query_index = base + lax.broadcasted_iota(jnp.int32, (1, count), 1)
    return (key_index <= query_index) & (key_index >= query_index - order_ref[0])


def key_probs(query, keys, allowed):
    scores = jnp.where(allowed, turned(keys, query) * HD**-0.5, -1e30)
    weights = jnp.exp(scores - jnp.max(scores, axis=0, keepdims=True))
    return weights * (1.0 / jnp.sum(weights, axis=0, keepdims=True))


def attend_kernel(base_ref, order_ref, query_ref, slots_ref, out_ref):
    count, keys = query_ref.shape[1], slots_ref.shape[1]
    allowed = allowed_keys(base_ref, order_ref, keys, count)
    key, value = slots_ref[0, :, :HD], slots_ref[0, :, HD:]
    parts = []
    for head in range(query_ref.shape[2] // HD):
        query = query_ref[0, :, head * HD : (head + 1) * HD]
        probs = key_probs(query, key, allowed)
        parts.append(summed(probs.astype(bf16), value))
    out_ref[0] = jnp.concatenate(parts, axis=1).astype(bf16)


def attend_back_kernel(base_ref, order_ref, query_ref, back_ref, slots_ref, back_query_ref, own_ref, rest_ref):
    count, keys = query_ref.shape[1], slots_ref.shape[1]
    allowed = allowed_keys(base_ref, order_ref, keys, count)
    key, value = slots_ref[0, :, :HD], slots_ref[0, :, HD:]
    back_queries = []
    back_key = jnp.zeros((keys, HD), f32)
    back_value = jnp.zeros((keys, HD), f32)
    for head in range(query_ref.shape[2] // HD):
        query = query_ref[0, :, head * HD : (head + 1) * HD]
        back = back_ref[0, :, head * HD : (head + 1) * HD]
        probs = key_probs(query, key, allowed)
        back_probs = turned(value, back)
        row_dot = jnp.sum(probs * back_probs, axis=0, keepdims=True)
        back_scores = (probs * (back_probs - row_dot)).astype(bf16)
        back_queries.append(summed(back_scores, key) * HD**-0.5)
        back_key += jnp.dot(back_scores, query, preferred_element_type=f32)
        back_value += jnp.dot(probs.astype(bf16), back, preferred_element_type=f32)
    back_query_ref[0] = jnp.concatenate(back_queries, axis=1)
    back_pair = jnp.concatenate([back_key * HD**-0.5, back_value], axis=1)
    own_ref[0] = back_pair[:count]
    rest_ref[0] = back_pair[count:].astype(bf16)


def attend_call(kernel, base, order, arrays, outs):
    sequences, count = order.shape

    def block(shape):
        return pl.BlockSpec((1,) + tuple(shape[1:]), lambda i: (i, 0, 0))

    keys = arrays[-1].shape[1]
    heads = arrays[0].shape[2] // HD
    return pl.pallas_call(
        kernel,
        grid=(sequences,),
        in_specs=[pl.BlockSpec(memory_space=pltpu.SMEM), block((sequences, 1, count))]
        + [block(array.shape) for array in arrays],
        out_specs=[block(out.shape) for out in outs],
        out_shape=outs,
        compiler_params=pltpu.CompilerParams(vmem_limit_bytes=56 * 1024 * 1024),
        cost_estimate=pl.CostEstimate(
            flops=10 * sequences * heads * count * keys * HD,
            bytes_accessed=sum(2 * array.size for array in arrays),
            transcendentals=sequences * heads * count * keys,
        ),
    )(base.reshape(1), order.reshape(sequences, 1, count), *arrays)


def attend_forward(team, core, hidden, order, gain, weights, query_gain, key_gain):
    inverse, normed, lowered = lowered_norm(hidden, gain)
    tokens = gather_tokens(team, lowered)
    heads = weights.shape[1] * 3 // 8 // HD
    groups = weights.shape[1] // 8 // HD
    repeat = heads // groups
    inner = (heads + 2 * groups) * HD
    mixed = true_order(core, team.size, project("td,dc->tc", tokens, weights[:, :inner]))
    sequences, count = mixed.shape[:2]
    query_heads = mixed[..., : heads * HD].reshape(sequences, count, heads, HD)
    key_heads = mixed[..., heads * HD : (heads + groups) * HD].reshape(sequences, count, groups, HD)
    value_low = mixed[..., (heads + groups) * HD :].astype(bf16)
    angles = order.astype(f32)[..., None] * frequencies()
    cosines, sines = jnp.cos(angles)[:, :, None, :], jnp.sin(angles)[:, :, None, :]
    query_inverse = rms_scale(query_heads)
    query_normed = query_heads * query_inverse
    query_rot = rotate(query_normed * query_gain, cosines, sines).astype(bf16)
    key_inverse = rms_scale(key_heads)
    key_normed = key_heads * key_inverse
    key_rot = rotate(key_normed * key_gain, cosines, sines).astype(bf16)
    pair = jnp.concatenate([key_rot.reshape(sequences, count, groups * HD), value_low], axis=-1)
    blocks = lax.axis_size("seq")
    here = lax.axis_index("seq")
    slots = jnp.concatenate([shift(pair, i) if i else pair for i in range(blocks)], axis=1)
    base = (here * count).astype(jnp.int32)
    query_rot = query_rot.reshape(sequences, count, heads * HD)
    (attended,) = attend_call(
        attend_kernel, base, order, [query_rot, slots], [jax.ShapeDtypeStruct((sequences, count, heads * HD), bf16)]
    )
    attended = own_halves(core, attended)
    out, sent = project_out(team, "tc,dc->td", attended, weights[:, inner:])
    stored = (
        inverse,
        normed,
        tokens,
        query_inverse,
        query_normed,
        key_inverse,
        key_normed,
        cosines,
        sines,
        query_rot,
        slots,
        base,
        order,
        attended,
    )
    return hidden + out, stored, mixed


def attend_backward(team, core, back_out, stored, gain, weights, query_gain, key_gain, before):
    (
        inverse,
        normed,
        tokens,
        query_inverse,
        query_normed,
        key_inverse,
        key_normed,
        cosines,
        sines,
        query_rot,
        slots,
        base,
        order,
        attended,
    ) = stored
    sequences, count = query_rot.shape[:2]
    heads, groups = query_rot.shape[2] // HD, slots.shape[2] // (2 * HD)
    inner = (heads + 2 * groups) * HD
    back_tokens = gather_tokens(team, back_out.astype(bf16))
    back_attended = true_order(core, team.size, project("td,dc->tc", back_tokens, held(weights[:, inner:], before[0]))).astype(bf16)
    back_query_rot, back_pair, rest = attend_call(
        attend_back_kernel,
        base,
        order,
        [query_rot, back_attended, slots],
        [
            jax.ShapeDtypeStruct((sequences, count, heads * HD), f32),
            jax.ShapeDtypeStruct((sequences, count, 2 * HD), f32),
            jax.ShapeDtypeStruct((sequences, slots.shape[1] - count, 2 * HD), bf16),
        ],
    )
    for i in range(1, slots.shape[1] // count):
        back_pair = back_pair + shift(rest[:, (i - 1) * count : i * count], -i).astype(f32)
    back_query_scaled = rotate(back_query_rot.reshape(sequences, count, heads, HD), cosines, -sines)
    query_scale_term = jnp.sum(back_query_scaled * query_normed, axis=(0, 1, 2))
    back_query = norm_back(back_query_scaled * query_gain, query_normed, query_inverse)
    back_key_rot = back_pair[..., : groups * HD].reshape(sequences, count, groups, HD)
    back_key_scaled = rotate(back_key_rot, cosines, -sines)
    key_scale_term = jnp.sum(back_key_scaled * key_normed, axis=(0, 1, 2))
    back_key = norm_back(back_key_scaled * key_gain, key_normed, key_inverse)
    back_mixed = jnp.concatenate(
        [
            back_query.reshape(sequences, count, heads * HD),
            back_key.reshape(sequences, count, groups * HD),
            back_pair[..., groups * HD :],
        ],
        axis=-1,
    ).astype(bf16)
    back_mixed = own_halves(core, back_mixed)
    back_normed, sent = project_out(team, "tc,dc->td", back_mixed, held(weights[:, :inner], before[1]))
    term = jnp.concatenate([outer(tokens, back_mixed), outer(back_tokens, attended)], axis=-1)
    back_hidden, gain_term = after_norm(back_out, back_normed, normed, inverse, gain)
    return back_hidden, gain_term, term, (query_scale_term, key_scale_term), back_attended


def grid_total(array):
    for axis in ("dp", "seq"):
        mask = 1
        while mask < lax.axis_size(axis):
            array = array + swap(array, axis, mask)
            mask *= 2
    return array


def body(
    hidden_in,
    positions,
    mixer_gain,
    mixer_in,
    mixer_taps,
    mixer_out,
    first_gain,
    first_lift,
    first_drop,
    attend_gain,
    query_weight,
    pair_weight,
    query_scale,
    key_scale,
    attend_out,
    second_gain,
    second_lift,
    second_drop,
    cotangent,
):
    core = lax.axis_index("mp")
    team = Team("dp")
    first_team = second_team = team
    rank = lax.axis_index("dp") * lax.axis_size("seq") + lax.axis_index("seq")
    model = hidden_in.shape[-1]
    share = hidden_in.shape[1] // 2
    own_tokens = lax.dynamic_slice_in_dim(hidden_in[0], core * share, share)
    hidden = own_tokens.astype(f32)
    signal_low = lax.dynamic_slice_in_dim(cotangent[0], core * share, share)
    signal = signal_low.astype(f32)
    query_gain, key_gain = query_scale.astype(f32), key_scale.astype(f32)
    channels = mixer_taps.shape[1] // team.size
    taps = lax.dynamic_slice_in_dim(mixer_taps, team.seat * channels, channels, 1).astype(f32)
    units = first_drop.shape[1]
    first_mask = hidden_mask(units, first_team.size, first_team.seat)
    second_mask = hidden_mask(units, second_team.size, second_team.seat)

    def feed_piece(on, lift, drop, late):
        width = hidden_width(units, on.size)

        def piece(seat):
            start = hidden_start(units, on.size, seat) + late
            parts = [lift[:, 0], lift[:, 1], drop]
            return jnp.concatenate([lax.dynamic_slice_in_dim(part, start, width, 1) for part in parts], axis=1)

        return piece

    def lift_of(pieces):
        return [piece[:, : 2 * piece.shape[1] // 3] for piece in pieces]

    def drop_of(pieces):
        return [piece[:, 2 * piece.shape[1] // 3 :] for piece in pieces]

    token_halves = gather_tokens(team, own_tokens)
    packed = pack_mixer(mixer_in, mixer_out)
    got = team_rows(team, lambda seat: take(packed, seat, 0))
    mixer_weights = all_rows(team, got)
    near_done = zero(got[-1])

    got_first = team_rows(first_team, feed_piece(first_team, first_lift, first_drop, near_done))
    first_lift_all = all_rows(first_team, lift_of(got_first))
    first_drop_all = all_rows(first_team, drop_of(got_first))
    near_done = zero(got_first[-1])

    gain_rows = mixer_gain.shape[0]
    gains = jnp.stack([mixer_gain, first_gain, attend_gain, second_gain]).astype(f32)
    gains = grid_total(
        lax.dynamic_update_slice_in_dim(jnp.zeros((4, model), f32), gains, rank * gain_rows + near_done, 1)
    )
    own_places = positions[0] + near_done
    order = jnp.stack([own_places] + [swap(own_places, team.axis, mask) for mask in range(1, team.size)])

    packed_attend = pack_attend(query_weight, pair_weight, attend_out)
    got_attend = team_rows(team, lambda seat: take(packed_attend, seat + near_done, 0))
    got_second = team_rows(second_team, feed_piece(second_team, second_lift, second_drop, near_done))

    after_mixer, mixer_stored, parts = mixer_forward(
        team, core, hidden, token_halves, order, gains[0], mixer_weights, taps
    )
    mixed_done = zero(parts)
    beside = [jnp.concatenate(pair, axis=1) for pair in zip(got_attend, drop_of(got_second))]
    shared = all_rows(team, beside, mixed_done)
    attend_weights, second_drop_all = shared[:, : got_attend[0].shape[1]], shared[:, got_attend[0].shape[1] :]
    second_lift_all = all_rows(second_team, lift_of(got_second), mixed_done)

    first_stored = feed_forward(first_team, after_mixer, gains[1], first_lift_all, first_mask)
    out, sent = project_out(first_team, "tf,df->td", first_stored[-1], first_drop_all)
    after_first = after_mixer + out
    after_attend, attend_stored, mixed = attend_forward(
        team, core, after_first, order, gains[2], attend_weights, query_gain, key_gain
    )
    signal_low = signal_low + zero(mixed).astype(bf16)
    signal_tokens = gather_tokens(second_team, signal_low)
    second_stored = feed_forward(second_team, after_attend, gains[3], second_lift_all, second_mask)

    result_sums, result_sends = scatter_begin(
        second_team, *project("tf,df->td", second_stored[-1], second_drop_all)
    )
    second_mask = held(second_mask, result_sends[-1][1])

    back, second_gain_term, *second_part = feed_backward(
        second_team, signal, signal_tokens, second_stored, gains[3], second_lift_all, second_drop_all, second_mask, None
    )
    back, attend_gain_term, attend_term, scale_terms, back_attended = attend_backward(
        team, core, back, attend_stored, gains[2], attend_weights, query_gain, key_gain, second_part
    )
    attend_part = summed_rows(team, attend_term)
    result = after_attend + scatter_end(second_team, held(result_sums, back_attended), result_sends)

    first_back_tokens = gather_tokens(first_team, back.astype(bf16))
    back, first_gain_term, *first_part = feed_backward(
        first_team, back, first_back_tokens, first_stored, gains[1], first_lift_all, first_drop_all, first_mask, attend_part
    )
    first_total = every_seat(first_team, jnp.concatenate(first_part[::-1], axis=-1))
    back, mixer_gain_term, mixer_term, tap_term, back_gated = mixer_backward(
        team, core, back, mixer_stored, gains[0], mixer_weights, taps, first_total
    )
    mixer_part = summed_rows(team, mixer_term)
    gated_done = zero(back_gated)
    second_total = every_seat(second_team, jnp.concatenate(second_part[::-1], axis=-1), gated_done)
    attend_total = every_seat(team, attend_part, gated_done)
    mixer_total = every_seat(team, mixer_part)

    small = jnp.concatenate(
        [mixer_gain_term, first_gain_term, attend_gain_term, second_gain_term, scale_terms[0], scale_terms[1]]
    )
    small = small + swap_core(small)
    tap_full = lax.dynamic_update_slice_in_dim(
        jnp.zeros((3, mixer_taps.shape[1]), f32), tap_term, team.seat * channels, 1
    )
    small = grid_total(jnp.concatenate([small, tap_full.reshape(-1)]))
    gain_totals = lax.dynamic_slice_in_dim(
        small[: 4 * model].reshape(4, model), rank * gain_rows, gain_rows, 1
    )
    scale_totals = small[4 * model : 4 * model + 2 * HD].reshape(2, HD)
    tap_total = small[4 * model + 2 * HD :].reshape(tap_full.shape)

    def both_cores(own):
        return true_order(core, 1, [own, swap_core(own)])

    def joined_lift(total):
        width = total.shape[-1] // 3
        return jnp.stack([joined_hidden(units, total[..., k * width : (k + 1) * width]) for k in range(2)], axis=1)

    def joined_drop(total):
        return joined_hidden(units, total[..., 2 * total.shape[-1] // 3 :])

    rows = mixer_in.shape[0]
    in_columns = 3 * channels
    inner = attend_total.shape[-1] - query_weight.shape[1] // 4
    queries = query_weight.shape[1] // 4
    return (
        both_cores(result.astype(bf16)),
        both_cores(back),
        gain_totals[0],
        all_seats(mixer_total[..., :in_columns].reshape(4, rows, 3, channels)),
        tap_total,
        all_seats(mixer_total[..., in_columns:]),
        gain_totals[1],
        joined_lift(first_total),
        joined_drop(first_total),
        gain_totals[2],
        all_seats(attend_total[..., :queries]),
        all_seats(attend_total[..., queries:inner].reshape(4, rows, 2, -1)),
        scale_totals[0],
        scale_totals[1],
        all_seats(attend_total[..., inner:]),
        gain_totals[3],
        joined_lift(second_total),
        joined_drop(second_total),
    )


def solution(mesh):
    grid = ("dp", "seq")
    return jax.shard_map(
        body,
        mesh=mesh,
        in_specs=(
            P("dp", "seq", None),
            P("dp", "seq"),
            P(grid),
            P(grid, None, "mp"),
            P(None, "mp"),
            P(grid, "mp"),
            P(grid),
            P(grid, None, "mp"),
            P(grid, "mp"),
            P(grid),
            P(grid, "mp"),
            P(grid, None, "mp"),
            P(),
            P(),
            P(grid, "mp"),
            P(grid),
            P(grid, None, "mp"),
            P(grid, "mp"),
            P("dp", "seq", None),
        ),
        out_specs=(
            P("dp", "seq", None),
            P("dp", "seq", None),
            P(grid),
            P(grid, None, "mp"),
            P(None, "mp"),
            P(grid, "mp"),
            P(grid),
            P(grid, None, "mp"),
            P(grid, "mp"),
            P(grid),
            P(grid, "mp"),
            P(grid, None, "mp"),
            P(),
            P(),
            P(grid, "mp"),
            P(grid),
            P(grid, None, "mp"),
            P(grid, "mp"),
        ),
        check_vma=False,
    )
```
